32 devices in a mesh: group: 2 (over x), ctx: 16 (over z, y, core).
Axes of the slice: x: 2, y: 2, z: 4, core: 2. Of those that a mesh axis runs over, the one named last changes fastest.
Arguments:
- queries: bfloat16 [256, 8, 8192], P(('group', 'ctx')), parts along dimension 0, may hold values from -40 to 40
- kv_cache: bfloat16 [32, 2, 512, 1024], P(('group', 'ctx')), parts along dimension 0, may hold values from -16 to 16
- page_counts: int32 [16], P('group'), parts along dimension 0, may hold values from 1 to 6, as said below
- doc_ids: int32 [16], P('group'), parts along dimension 0, may hold values from 0 to 7, each once
Outputs:
- attended: bfloat16 [256, 8, 8192], P(('group', 'ctx')), parts along dimension 0
The draws below stay inside these ranges and needn't reach their ends.
There are 2 independent parts, one for each index of `group`. The reference program is written for one: setup_inputs(seed, part) draws one part's arguments, and reference() takes and returns one part's arrays. A program takes and returns all parts, laid end to end along the dimension named above; each array names one. Nothing has to cross between parts.
Inputs may be any that keep to these rules, and one draw needn't show every extreme that they name: `page_counts`: the counts sum to 16; every document holds at least 1 pages, some document exactly 1, and some document exactly 6. `doc_ids`: every document is named by exactly one question block.
All inputs are finite; a program needn't handle non-finite values.
Results may differ from the reference program's by a relative error of at most 0.0031.
Values may be sent and summed in bfloat16 or wider, within the bound.
No kernel may reach another device: no remote copies, remote signals or barrier semaphores. Data moves between devices by JAX's collectives and lax.ppermute only.
A program may use at most 128 MiB of HBM per device.

```python
import jax
import jax.numpy as jnp
from jax import lax

HEADS = 64
KV_HEADS = 8
HEAD_DIM = 128
DOCS = 8
QUERY_TOK = 128
PAGE_TOK = 512
PAGES_DEV = 1
PAGES = 16


def draw_queries(key, part):
    width = HEADS * HEAD_DIM
    base = jax.random.truncated_normal(jax.random.fold_in(key, 21), -4.0, 4.0, (QUERY_TOK, DOCS, width), jnp.float32) * 2.0
    return base.astype(jnp.bfloat16)


def draw_kv_cache(key, part):
    noise = jax.random.truncated_normal(jax.random.fold_in(key, 31), -4.0, 4.0, (PAGES, 2, PAGE_TOK, KV_HEADS * HEAD_DIM), jnp.float32)
    key_part = noise[:, 0]
    value_part = 4.0 * noise[:, 1]
    return jnp.stack([key_part, value_part], axis=1).astype(jnp.bfloat16)


def draw_page_counts(key, part):
    most_pages = 3 * PAGES // DOCS
    middle = DOCS - 2
    rest_pages = PAGES - most_pages - PAGES_DEV
    extra_pages = rest_pages - middle * PAGES_DEV
    share_base = extra_pages // middle
    leftover = extra_pages % middle
    shares = share_base + (jnp.arange(middle, dtype=jnp.int32) < leftover).astype(jnp.int32)
    pair_count = middle // 2
    spread = max(0, min(share_base, most_pages - PAGES_DEV - share_base - 1))
    delta = jax.random.randint(jax.random.fold_in(key, 43), (pair_count,), 0, spread + 1).astype(jnp.int32)
    moved = jnp.zeros((middle,), jnp.int32)
    moved = moved.at[0:2 * pair_count:2].add(delta)
    moved = moved.at[1:2 * pair_count:2].add(-delta)
    middle_counts = PAGES_DEV + shares + moved
    counts = jnp.concatenate([jnp.full((1,), most_pages, jnp.int32), jnp.full((1,), PAGES_DEV, jnp.int32), middle_counts])
    shuffle = jax.random.permutation(jax.random.fold_in(key, 42), DOCS)
    return counts[shuffle].astype(jnp.int32)


def setup_inputs(seed: int = 0, part: int = 0) -> dict:
    key_list = jax.random.split(jax.random.key(seed), 5)
    own_keys = jax.random.split(jax.random.fold_in(key_list[4], part), 5)
    return {
        "queries": draw_queries(jax.random.fold_in(jax.random.fold_in(key_list[4], part), 71), part),
        "kv_cache": draw_kv_cache(jax.random.fold_in(jax.random.fold_in(key_list[4], part), 71), part),
        "page_counts": draw_page_counts(jax.random.fold_in(jax.random.fold_in(key_list[4], part), 71), part),
        "doc_ids": jax.random.permutation(own_keys[3], DOCS).astype(jnp.int32),
    }


def page_partial(rows, page_kv):
    tokens = rows.shape[0]
    kv_heads = page_kv.shape[-1] // HEAD_DIM
    groups = rows.shape[-1] // (kv_heads * HEAD_DIM)
    grouped = rows.astype(jnp.float32).reshape(tokens, kv_heads, groups, HEAD_DIM)
    keys = page_kv[0].astype(jnp.float32).reshape(-1, kv_heads, HEAD_DIM)
    values = page_kv[1].astype(jnp.float32).reshape(-1, kv_heads, HEAD_DIM)
    scores = jnp.einsum("qhgd,khd->qhgk", grouped, keys, precision=lax.Precision.HIGHEST) * (HEAD_DIM ** -0.5)
    row_max = jnp.max(scores, axis=-1)
    expo = jnp.exp(scores - row_max[..., None])
    row_sum = jnp.sum(expo, axis=-1)
    weights = lax.optimization_barrier(expo.astype(jnp.bfloat16)).astype(jnp.float32)
    mixed = jnp.einsum("qhgk,khd->qhgd", weights, values, precision=lax.Precision.HIGHEST)
    return row_max.reshape(tokens, -1), row_sum.reshape(tokens, -1), mixed.reshape(tokens, -1)


def reference(queries, kv_cache, page_counts, doc_ids):
    doc_ends = jnp.cumsum(page_counts).astype(jnp.int32)
    block_order = jnp.arange(DOCS, dtype=jnp.int32)
    width = HEADS * HEAD_DIM

    def visit(carry, page):
        big_max, big_sum, big_out = carry
        page_doc = jnp.sum((page >= doc_ends).astype(jnp.int32))
        block = jnp.sum(jnp.where(doc_ids == page_doc, block_order, 0)).astype(jnp.int32)
        rows = lax.dynamic_index_in_dim(queries, block, 1, keepdims=False)
        page_kv = lax.dynamic_index_in_dim(kv_cache, page.astype(jnp.int32), 0, keepdims=False)
        row_max, row_sum, mixed = page_partial(rows, page_kv)
        old_max = lax.dynamic_index_in_dim(big_max, block, 0, keepdims=False)
        old_sum = lax.dynamic_index_in_dim(big_sum, block, 0, keepdims=False)
        old_out = lax.dynamic_index_in_dim(big_out, block, 0, keepdims=False)
        new_max = jnp.maximum(old_max, row_max)
        keep_old = jnp.exp(old_max - new_max)
        keep_new = jnp.exp(row_max - new_max)
        new_sum = keep_old * old_sum + keep_new * row_sum
        tokens = rows.shape[0]
        new_out = (keep_old[..., None] * old_out.reshape(tokens, HEADS, HEAD_DIM)
                   + keep_new[..., None] * mixed.reshape(tokens, HEADS, HEAD_DIM)).reshape(tokens, width)
        big_max = lax.dynamic_update_index_in_dim(big_max, new_max, block, 0)
        big_sum = lax.dynamic_update_index_in_dim(big_sum, new_sum, block, 0)
        big_out = lax.dynamic_update_index_in_dim(big_out, new_out, block, 0)
        return (big_max, big_sum, big_out), None

    start = (jnp.full((DOCS, QUERY_TOK, HEADS), -1e30, jnp.float32),
             jnp.zeros((DOCS, QUERY_TOK, HEADS), jnp.float32),
             jnp.zeros((DOCS, QUERY_TOK, width), jnp.float32))
    pages = jnp.arange(PAGES, dtype=jnp.int32)
    (big_max, big_sum, big_out), unused = lax.scan(visit, start, pages)
    normed = big_out.reshape(DOCS, QUERY_TOK, HEADS, HEAD_DIM) / big_sum[..., None]
    normed = jnp.transpose(normed.reshape(DOCS, QUERY_TOK, width), (1, 0, 2))
    return normed.astype(jnp.bfloat16)
```

```python
import jax
import jax.numpy as jnp
from jax import lax
from jax.sharding import PartitionSpec as P

HEAD_DIM = 128


def doc_of(pages, doc_ends):
    return jnp.sum((pages[..., None] >= doc_ends).astype(jnp.int32), axis=-1)


def page_partial(rows, page_kv):
    tokens = rows.shape[0]
    kv_heads = page_kv.shape[-1] // HEAD_DIM
    groups = rows.shape[-1] // (kv_heads * HEAD_DIM)
    grouped = rows.reshape(tokens, kv_heads, groups, HEAD_DIM)
    keys = page_kv[0].reshape(-1, kv_heads, HEAD_DIM)
    values = page_kv[1].reshape(-1, kv_heads, HEAD_DIM)
    scores = jnp.einsum(
        "qhgd,khd->qhgk", grouped, keys, preferred_element_type=jnp.float32
    ) * HEAD_DIM ** (-0.5)
    row_max = jnp.max(scores, axis=-1)
    expo = jnp.exp(scores - row_max[..., None])
    row_sum = jnp.sum(expo, axis=-1)
    weights = expo.astype(jnp.bfloat16)
    mixed = jnp.einsum("qhgk,khd->qhgd", weights, values, preferred_element_type=jnp.float32)
    return (row_max.reshape(tokens, -1), row_sum.reshape(tokens, -1), mixed.reshape(tokens, -1))


def page_blocks(pages, page_counts, doc_ids):
    block_order = jnp.arange(doc_ids.shape[0], dtype=jnp.int32)
    page_docs = doc_of(pages, jnp.cumsum(page_counts))
    return jnp.sum(jnp.where(doc_ids == page_docs[:, None], block_order, 0), axis=-1)


def body(queries, kv_cache, page_counts, doc_ids):
    peers = lax.axis_size("ctx")
    local_rows, blocks, width = queries.shape
    heads = width // HEAD_DIM
    block_of = page_blocks(jnp.arange(peers, dtype=jnp.int32), page_counts, doc_ids)
    outgoing = jnp.take(queries, block_of, axis=1)
    arrived = lax.all_to_all(outgoing, "ctx", split_axis=1, concat_axis=0, tiled=True)
    row_max, row_sum, mixed = page_partial(arrived.reshape(-1, width), kv_cache[0])
    send = [part.reshape(peers, local_rows, -1) for part in (mixed, row_max, row_sum)]
    got_out, got_max, got_sum = [
        lax.all_to_all(part, "ctx", split_axis=0, concat_axis=0, tiled=True) for part in send
    ]
    matches = (block_of == jnp.arange(blocks, dtype=jnp.int32)[:, None])[..., None, None]
    masked = jnp.where(matches, got_max, -1e30)
    row_top = jnp.max(masked, axis=1, keepdims=True)
    weight = jnp.where(matches, jnp.exp(masked - row_top), 0.0)
    denominator = jnp.sum(weight * got_sum, axis=1)
    numerator = jnp.einsum(
        "cnrh,nrhd->crhd",
        weight,
        got_out.reshape(peers, local_rows, heads, HEAD_DIM),
        precision=lax.Precision.HIGHEST,
    )
    mixed_out = (numerator / denominator[..., None]).reshape(blocks, local_rows, width)
    return jnp.moveaxis(mixed_out, 0, 1).astype(jnp.bfloat16)


def solution(mesh):
    placed = (
        P(("group", "ctx"), None, None),
        P(("group", "ctx"), None, None, None),
        P("group"),
        P("group"),
    )
    return jax.shard_map(
        body, mesh=mesh, in_specs=placed, out_specs=P(("group", "ctx"), None, None), check_vma=False
    )
```

```python
import functools
import math

import jax
import jax.numpy as jnp
from jax import lax
from jax.experimental import pallas as pl
from jax.experimental.pallas import tpu as pltpu
from jax.sharding import PartitionSpec as P

HEAD_DIM = 128
TILE = 8
STAT_ROWS = 16
VMEM_BYTES = 32 * 1024 * 1024


def doc_of(pages, doc_ends):
    return jnp.sum((pages[..., None] >= doc_ends).astype(jnp.int32), axis=-1)


def page_partial(rows, page_kv):
    tokens = rows.shape[0]
    kv_heads = page_kv.shape[-1] // HEAD_DIM
    groups = rows.shape[-1] // (kv_heads * HEAD_DIM)
    grouped = rows.reshape(tokens, kv_heads, groups, HEAD_DIM)
    keys = page_kv[0].reshape(-1, kv_heads, HEAD_DIM)
    values = page_kv[1].reshape(-1, kv_heads, HEAD_DIM)
    scores = jnp.einsum(
        "qhgd,khd->qhgk", grouped, keys, preferred_element_type=jnp.float32
    ) * HEAD_DIM ** (-0.5)
    row_max = jnp.max(scores, axis=-1)
    expo = jnp.exp(scores - row_max[..., None])
    row_sum = jnp.sum(expo, axis=-1)
    weights = expo.astype(jnp.bfloat16)
    mixed = jnp.einsum("qhgk,khd->qhgd", weights, values, preferred_element_type=jnp.float32)
    return (row_max.reshape(tokens, -1), row_sum.reshape(tokens, -1), mixed.reshape(tokens, -1))


def page_blocks(pages, page_counts, doc_ids):
    block_order = jnp.arange(doc_ids.shape[0], dtype=jnp.int32)
    page_docs = doc_of(pages, jnp.cumsum(page_counts))
    return jnp.sum(jnp.where(doc_ids == page_docs[:, None], block_order, 0), axis=-1)


def gathered_body(queries, kv_cache, page_counts, doc_ids):
    peers = lax.axis_size("ctx")
    local_rows, blocks, width = queries.shape
    heads = width // HEAD_DIM
    block_of = page_blocks(jnp.arange(peers, dtype=jnp.int32), page_counts, doc_ids)
    outgoing = jnp.take(queries, block_of, axis=1)
    arrived = lax.all_to_all(outgoing, "ctx", split_axis=1, concat_axis=0, tiled=True)
    row_max, row_sum, mixed = page_partial(arrived.reshape(-1, width), kv_cache[0])
    send = [part.reshape(peers, local_rows, -1) for part in (mixed, row_max, row_sum)]
    got_out, got_max, got_sum = [
        lax.all_to_all(part, "ctx", split_axis=0, concat_axis=0, tiled=True) for part in send
    ]
    matches = (block_of == jnp.arange(blocks, dtype=jnp.int32)[:, None])[..., None, None]
    masked = jnp.where(matches, got_max, -1e30)
    row_top = jnp.max(masked, axis=1, keepdims=True)
    weight = jnp.where(matches, jnp.exp(masked - row_top), 0.0)
    denominator = jnp.sum(weight * got_sum, axis=1)
    numerator = jnp.einsum(
        "cnrh,nrhd->crhd",
        weight,
        got_out.reshape(peers, local_rows, heads, HEAD_DIM),
        precision=lax.Precision.HIGHEST,
    )
    mixed_out = (numerator / denominator[..., None]).reshape(blocks, local_rows, width)
    return jnp.moveaxis(mixed_out, 0, 1).astype(jnp.bfloat16)


def pack_kernel(count, block_ref, query_ref, *sent_refs):
    tokens, blocks, width = query_ref.shape
    row = lax.broadcasted_iota(jnp.int32, (tokens, tokens * blocks), 0)
    column = lax.broadcasted_iota(jnp.int32, (tokens, tokens * blocks), 1)
    pick = jnp.concatenate(
        [jnp.where(column == row * blocks + block_ref[n], 1.0, 0.0) for n in range(count)], axis=0
    ).astype(jnp.bfloat16)
    part = TILE * HEAD_DIM
    for head in range(width // part):
        span = slice(head * part, (head + 1) * part)
        rows = jnp.concatenate(
            [query_ref[t, :, span].astype(jnp.float32) for t in range(tokens)], axis=0
        ).astype(jnp.bfloat16)
        picked = jnp.dot(pick, rows, preferred_element_type=jnp.float32)
        for n in range(count):
            own = picked[n * tokens : (n + 1) * tokens]
            own = jnp.concatenate(
                [own[:, g * HEAD_DIM : (g + 1) * HEAD_DIM] for g in range(TILE)], axis=0
            )
            size = TILE * tokens
            sent_refs[n][head * size : (head + 1) * size, :] = own.astype(jnp.bfloat16)


def pack_queries(queries, block_of):
    count = block_of.shape[0]
    tokens, _, width = queries.shape
    rows = tokens * width // HEAD_DIM
    return pl.pallas_call(
        functools.partial(pack_kernel, count),
        out_shape=[jax.ShapeDtypeStruct((rows, HEAD_DIM), jnp.bfloat16)] * count,
        in_specs=[pl.BlockSpec(memory_space=pltpu.SMEM), pl.BlockSpec(memory_space=pltpu.VMEM)],
        out_specs=[pl.BlockSpec(memory_space=pltpu.VMEM)] * count,
        compiler_params=pltpu.CompilerParams(vmem_limit_bytes=VMEM_BYTES),
        cost_estimate=pl.CostEstimate(flops=0, bytes_accessed=4 << 20, transcendentals=0),
        name="pack_queries",
    )(block_of, queries)


def attend_kernel(count, kv_ref, *refs):
    asked, answers, log_ref = refs[:count], refs[count : 2 * count], refs[2 * count]
    kv_heads = kv_ref.shape[2] // HEAD_DIM
    size = asked[0].shape[0] // kv_heads
    scale = HEAD_DIM ** (-0.5)

    def one_head(head, carry):
        lanes = pl.ds(pl.multiple_of(head * HEAD_DIM, HEAD_DIM), HEAD_DIM)
        rows = pl.ds(pl.multiple_of(head * size, size), size)
        keys, values = kv_ref[0, :, lanes], kv_ref[1, :, lanes]
        query = jnp.concatenate([ref[rows, :] for ref in asked], axis=0)
        scores = lax.dot_general(
            keys, query, (((1,), (1,)), ((), ())), preferred_element_type=jnp.float32
        )
        top = jnp.max(scores, axis=0, keepdims=True)
        expo = jnp.exp2((scores - top) * (scale / math.log(2.0)))
        total = jnp.sum(expo, axis=0, keepdims=True)
        mixed = lax.dot_general(
            values,
            expo.astype(jnp.bfloat16),
            (((0,), (0,)), ((), ())),
            preferred_element_type=jnp.float32,
        )
        mixed = jnp.transpose(mixed * (1.0 / total))
        for n in range(count):
            answers[n][rows, :] = mixed[n * size : (n + 1) * size].astype(jnp.bfloat16)
        log_ref[pl.ds(head, 1), :] = top * scale + jnp.log(total)
        return carry

    lax.fori_loop(0, kv_heads, one_head, 0)
    logs = log_ref[...]
    high = logs.astype(jnp.bfloat16).astype(jnp.float32)
    middle = (logs - high).astype(jnp.bfloat16).astype(jnp.float32)
    low = logs - high - middle
    for n in range(count):
        span = slice(n * size, (n + 1) * size)
        upper = jnp.concatenate([high[:, span], middle[:, span]], axis=1)
        lower = jnp.concatenate([low[:, span], jnp.zeros_like(low[:, span])], axis=1)
        answers[n][kv_heads * size :, :] = jnp.concatenate([upper, lower], axis=0).astype(
            jnp.bfloat16
        )


def attend_page(page_kv, asked):
    count = len(asked)
    rows = asked[0].shape[0]
    kv_heads = page_kv.shape[2] // HEAD_DIM
    flops = 4 * count * rows * page_kv.shape[1] * HEAD_DIM
    return pl.pallas_call(
        functools.partial(attend_kernel, count),
        out_shape=[jax.ShapeDtypeStruct((rows + STAT_ROWS, HEAD_DIM), jnp.bfloat16)] * count,
        in_specs=[pl.BlockSpec(memory_space=pltpu.VMEM)] * (1 + count),
        out_specs=[pl.BlockSpec(memory_space=pltpu.VMEM)] * count,
        scratch_shapes=[pltpu.VMEM((kv_heads, count * rows // kv_heads), jnp.float32)],
        compiler_params=pltpu.CompilerParams(vmem_limit_bytes=VMEM_BYTES),
        cost_estimate=pl.CostEstimate(
            flops=flops, bytes_accessed=3 << 20, transcendentals=flops // 512
        ),
        name="attend_page",
    )(page_kv, *asked)


def merge_kernel(count, block_ref, *refs):
    parts, out_ref, sum_ref, top_ref, total_ref = refs[:count], *refs[count:]
    tokens, blocks, width = out_ref.shape
    size = TILE * tokens
    kv_heads = width // (TILE * HEAD_DIM)
    top_ref[...] = jnp.full(top_ref.shape, -1e30, jnp.float32)
    total_ref[...] = jnp.zeros(total_ref.shape, jnp.float32)
    sum_ref[...] = jnp.zeros(sum_ref.shape, jnp.float32)
    logs = []
    for n in range(count):
        stat = parts[n][kv_heads * size :, :].astype(jnp.float32)
        log = stat[:kv_heads, :size] + stat[:kv_heads, size:] + stat[kv_heads:, :size]
        logs.append(log)
        top_ref[block_ref[n]] = jnp.maximum(top_ref[block_ref[n]], log)
    shares = [jnp.exp(logs[n] - top_ref[block_ref[n]]) for n in range(count)]
    for n in range(count):
        total_ref[block_ref[n]] += shares[n]
    shares = jnp.concatenate([shares[n] / total_ref[block_ref[n]] for n in range(count)], axis=0)
    shares = jnp.concatenate([shares, jnp.zeros_like(shares)], axis=1)
    columns = jnp.transpose(shares)
    for n in range(count):
        for head in range(kv_heads):
            rows = slice(head * size, (head + 1) * size)
            place = n * kv_heads + head
            share = columns[:size, place : place + 1]
            sum_ref[block_ref[n], rows, :] += share * parts[n][rows, :].astype(jnp.float32)
    row = lax.broadcasted_iota(jnp.int32, (tokens * blocks, tokens * blocks), 0)
    column = lax.broadcasted_iota(jnp.int32, (tokens * blocks, tokens * blocks), 1)
    turned = (row // blocks == column % tokens) & (row % blocks == column // tokens)
    turn = jnp.where(turned, 1.0, 0.0).astype(jnp.bfloat16)
    part = TILE * HEAD_DIM
    for head in range(kv_heads):
        lanes = []
        for g in range(TILE):
            first = head * size + g * tokens
            lanes.append(
                jnp.concatenate(
                    [sum_ref[b, first : first + tokens, :] for b in range(blocks)], axis=0
                )
            )
        block_rows = jnp.concatenate(lanes, axis=1).astype(jnp.bfloat16)
        token_rows = jnp.dot(turn, block_rows, preferred_element_type=jnp.float32)
        for t in range(tokens):
            out_ref[t, :, head * part : (head + 1) * part] = token_rows[
                t * blocks : (t + 1) * blocks
            ].astype(jnp.bfloat16)


def merge_pages(block_of, parts, like):
    count = len(parts)
    tokens, blocks, width = like.shape
    kv_heads = width // (TILE * HEAD_DIM)
    size = TILE * tokens
    return pl.pallas_call(
        functools.partial(merge_kernel, count),
        out_shape=jax.ShapeDtypeStruct(like.shape, jnp.bfloat16),
        in_specs=[pl.BlockSpec(memory_space=pltpu.SMEM)]
        + [pl.BlockSpec(memory_space=pltpu.VMEM)] * count,
        out_specs=pl.BlockSpec(memory_space=pltpu.VMEM),
        scratch_shapes=[
            pltpu.VMEM((blocks, kv_heads * size, HEAD_DIM), jnp.float32),
            pltpu.VMEM((blocks, kv_heads, size), jnp.float32),
            pltpu.VMEM((blocks, kv_heads, size), jnp.float32),
        ],
        compiler_params=pltpu.CompilerParams(vmem_limit_bytes=VMEM_BYTES),
        cost_estimate=pl.CostEstimate(flops=0, bytes_accessed=4 << 20, transcendentals=0),
        name="merge_pages",
    )(block_of, *parts)


def swapped(value, step):
    if step == 0:
        return value
    count = lax.axis_size("ctx")
    return lax.ppermute(value, "ctx", [(source, source ^ step) for source in range(count)])


def stepped_body(queries, kv_cache, page_counts, doc_ids):
    peers = lax.axis_size("ctx")
    pages = lax.axis_index("ctx") ^ jnp.arange(peers, dtype=jnp.int32)
    block_of = page_blocks(pages, page_counts, doc_ids)
    half, quarter = peers // 2, peers // 4
    asked = {}
    for first in (half, 0):
        steps = range(first, first + half)
        for step, sent in zip(steps, pack_queries(queries, block_of[first : first + half])):
            asked[step] = swapped(sent, step)
    parts = {}
    for first in (2 * quarter, 3 * quarter, quarter, 0):
        steps = range(first, first + quarter)
        for step, answer in zip(steps, attend_page(kv_cache[0], [asked[s] for s in steps])):
            parts[step] = swapped(answer, step)
    return merge_pages(block_of, [parts[step] for step in range(peers)], queries)


def body(queries, kv_cache, page_counts, doc_ids):
    tokens, blocks, width = queries.shape
    groups = width // kv_cache.shape[-1]
    fits = tokens == TILE and blocks == TILE and groups == TILE and lax.axis_size("ctx") == 2 * TILE
    chosen = stepped_body if fits else gathered_body
    return chosen(queries, kv_cache, page_counts, doc_ids)


def solution(mesh):
    placed = (
        P(("group", "ctx"), None, None),
        P(("group", "ctx"), None, None, None),
        P("group"),
        P("group"),
    )
    return jax.shard_map(
        body, mesh=mesh, in_specs=placed, out_specs=P(("group", "ctx"), None, None), check_vma=False
    )
```

```python
import functools
import math

import jax
import jax.numpy as jnp
from jax import lax
from jax.experimental import pallas as pl
from jax.experimental.pallas import tpu as pltpu
from jax.sharding import PartitionSpec as P

HEAD_DIM = 128
TILE = 8
STAT_ROWS = 16
VMEM_BYTES = 32 * 1024 * 1024


def doc_of(pages, doc_ends):
    return jnp.sum((pages[..., None] >= doc_ends).astype(jnp.int32), axis=-1)


def page_partial(rows, page_kv):
    tokens = rows.shape[0]
    kv_heads = page_kv.shape[-1] // HEAD_DIM
    groups = rows.shape[-1] // (kv_heads * HEAD_DIM)
    grouped = rows.reshape(tokens, kv_heads, groups, HEAD_DIM)
    keys = page_kv[0].reshape(-1, kv_heads, HEAD_DIM)
    values = page_kv[1].reshape(-1, kv_heads, HEAD_DIM)
    scores = jnp.einsum(
        "qhgd,khd->qhgk", grouped, keys, preferred_element_type=jnp.float32
    ) * HEAD_DIM ** (-0.5)
    row_max = jnp.max(scores, axis=-1)
    expo = jnp.exp(scores - row_max[..., None])
    row_sum = jnp.sum(expo, axis=-1)
    weights = expo.astype(jnp.bfloat16)
    mixed = jnp.einsum("qhgk,khd->qhgd", weights, values, preferred_element_type=jnp.float32)
    return (row_max.reshape(tokens, -1), row_sum.reshape(tokens, -1), mixed.reshape(tokens, -1))


def page_blocks(pages, page_counts, doc_ids):
    block_order = jnp.arange(doc_ids.shape[0], dtype=jnp.int32)
    page_docs = doc_of(pages, jnp.cumsum(page_counts))
    return jnp.sum(jnp.where(doc_ids == page_docs[:, None], block_order, 0), axis=-1)


def gathered_body(queries, kv_cache, page_counts, doc_ids):
    peers = lax.axis_size("ctx")
    local_rows, blocks, width = queries.shape
    heads = width // HEAD_DIM
    block_of = page_blocks(jnp.arange(peers, dtype=jnp.int32), page_counts, doc_ids)
    outgoing = jnp.take(queries, block_of, axis=1)
    arrived = lax.all_to_all(outgoing, "ctx", split_axis=1, concat_axis=0, tiled=True)
    row_max, row_sum, mixed = page_partial(arrived.reshape(-1, width), kv_cache[0])
    send = [part.reshape(peers, local_rows, -1) for part in (mixed, row_max, row_sum)]
    got_out, got_max, got_sum = [
        lax.all_to_all(part, "ctx", split_axis=0, concat_axis=0, tiled=True) for part in send
    ]
    matches = (block_of == jnp.arange(blocks, dtype=jnp.int32)[:, None])[..., None, None]
    masked = jnp.where(matches, got_max, -1e30)
    row_top = jnp.max(masked, axis=1, keepdims=True)
    weight = jnp.where(matches, jnp.exp(masked - row_top), 0.0)
    denominator = jnp.sum(weight * got_sum, axis=1)
    numerator = jnp.einsum(
        "cnrh,nrhd->crhd",
        weight,
        got_out.reshape(peers, local_rows, heads, HEAD_DIM),
        precision=lax.Precision.HIGHEST,
    )
    mixed_out = (numerator / denominator[..., None]).reshape(blocks, local_rows, width)
    return jnp.moveaxis(mixed_out, 0, 1).astype(jnp.bfloat16)


def pack_kernel(count, block_ref, query_ref, *sent_refs):
    tokens, blocks, width = query_ref.shape
    row = lax.broadcasted_iota(jnp.int32, (tokens, tokens * blocks), 0)
    column = lax.broadcasted_iota(jnp.int32, (tokens, tokens * blocks), 1)
    pick = jnp.concatenate(
        [jnp.where(column == row * blocks + block_ref[n], 1.0, 0.0) for n in range(count)], axis=0
    ).astype(jnp.bfloat16)
    part = TILE * HEAD_DIM
    for head in range(width // part):
        span = slice(head * part, (head + 1) * part)
        rows = jnp.concatenate(
            [query_ref[t, :, span].astype(jnp.float32) for t in range(tokens)], axis=0
        ).astype(jnp.bfloat16)
        picked = jnp.dot(pick, rows, preferred_element_type=jnp.float32)
        for n in range(count):
            own = picked[n * tokens : (n + 1) * tokens]
            own = jnp.concatenate(
                [own[:, g * HEAD_DIM : (g + 1) * HEAD_DIM] for g in range(TILE)], axis=0
            )
            size = TILE * tokens
            sent_refs[n][head * size : (head + 1) * size, :] = own.astype(jnp.bfloat16)


def pack_queries(queries, block_of):
    count = block_of.shape[0]
    tokens, _, width = queries.shape
    rows = tokens * width // HEAD_DIM
    return pl.pallas_call(
        functools.partial(pack_kernel, count),
        out_shape=[jax.ShapeDtypeStruct((rows, HEAD_DIM), jnp.bfloat16)] * count,
        in_specs=[pl.BlockSpec(memory_space=pltpu.SMEM), pl.BlockSpec(memory_space=pltpu.VMEM)],
        out_specs=[pl.BlockSpec(memory_space=pltpu.VMEM)] * count,
        compiler_params=pltpu.CompilerParams(vmem_limit_bytes=VMEM_BYTES),
        cost_estimate=pl.CostEstimate(flops=0, bytes_accessed=4 << 20, transcendentals=0),
        name="pack_queries",
    )(block_of, queries)


def attend_kernel(count, kv_ref, *refs):
    asked, answers, log_ref = refs[:count], refs[count : 2 * count], refs[2 * count]
    kv_heads = kv_ref.shape[2] // HEAD_DIM
    size = asked[0].shape[0] // kv_heads
    scale = HEAD_DIM ** (-0.5)

    def one_head(head, carry):
        lanes = pl.ds(pl.multiple_of(head * HEAD_DIM, HEAD_DIM), HEAD_DIM)
        rows = pl.ds(pl.multiple_of(head * size, size), size)
        keys, values = kv_ref[0, :, lanes], kv_ref[1, :, lanes]
        query = jnp.concatenate([ref[rows, :] for ref in asked], axis=0)
        scores = lax.dot_general(
            keys, query, (((1,), (1,)), ((), ())), preferred_element_type=jnp.float32
        )
        top = jnp.max(scores, axis=0, keepdims=True)
        expo = jnp.exp2((scores - top) * (scale / math.log(2.0)))
        total = jnp.sum(expo, axis=0, keepdims=True)
        mixed = lax.dot_general(
            values,
            expo.astype(jnp.bfloat16),
            (((0,), (0,)), ((), ())),
            preferred_element_type=jnp.float32,
        )
        mixed = jnp.transpose(mixed * (1.0 / total))
        for n in range(count):
            answers[n][rows, :] = mixed[n * size : (n + 1) * size].astype(jnp.bfloat16)
        log_ref[pl.ds(head, 1), :] = top * scale + jnp.log(total)
        return carry

    lax.fori_loop(0, kv_heads, one_head, 0)
    logs = log_ref[...]
    high = logs.astype(jnp.bfloat16).astype(jnp.float32)
    middle = (logs - high).astype(jnp.bfloat16).astype(jnp.float32)
    low = logs - high - middle
    for n in range(count):
        span = slice(n * size, (n + 1) * size)
        upper = jnp.concatenate([high[:, span], middle[:, span]], axis=1)
        lower = jnp.concatenate([low[:, span], jnp.zeros_like(low[:, span])], axis=1)
        answers[n][kv_heads * size :, :] = jnp.concatenate([upper, lower], axis=0).astype(
            jnp.bfloat16
        )


def attend_page(page_kv, asked):
    count = len(asked)
    rows = asked[0].shape[0]
    kv_heads = page_kv.shape[2] // HEAD_DIM
    flops = 4 * count * rows * page_kv.shape[1] * HEAD_DIM
    return pl.pallas_call(
        functools.partial(attend_kernel, count),
        out_shape=[jax.ShapeDtypeStruct((rows + STAT_ROWS, HEAD_DIM), jnp.bfloat16)] * count,
        in_specs=[pl.BlockSpec(memory_space=pltpu.VMEM)] * (1 + count),
        out_specs=[pl.BlockSpec(memory_space=pltpu.VMEM)] * count,
        scratch_shapes=[pltpu.VMEM((kv_heads, count * rows // kv_heads), jnp.float32)],
        compiler_params=pltpu.CompilerParams(vmem_limit_bytes=VMEM_BYTES),
        cost_estimate=pl.CostEstimate(
            flops=flops, bytes_accessed=3 << 20, transcendentals=flops // 512
        ),
        name="attend_page",
    )(page_kv, *asked)


def merge_kernel(count, block_ref, *refs):
    parts, out_ref, sum_ref, top_ref, total_ref = refs[:count], *refs[count:]
    tokens, blocks, width = out_ref.shape
    size = TILE * tokens
    kv_heads = width // (TILE * HEAD_DIM)
    top_ref[...] = jnp.full(top_ref.shape, -1e30, jnp.float32)
    total_ref[...] = jnp.zeros(total_ref.shape, jnp.float32)
    sum_ref[...] = jnp.zeros(sum_ref.shape, jnp.float32)
    logs = []
    for n in range(count):
        stat = parts[n][kv_heads * size :, :].astype(jnp.float32)
        log = stat[:kv_heads, :size] + stat[:kv_heads, size:] + stat[kv_heads:, :size]
        logs.append(log)
        top_ref[block_ref[n]] = jnp.maximum(top_ref[block_ref[n]], log)
    shares = [jnp.exp(logs[n] - top_ref[block_ref[n]]) for n in range(count)]
    for n in range(count):
        total_ref[block_ref[n]] += shares[n]
    shares = jnp.concatenate([shares[n] / total_ref[block_ref[n]] for n in range(count)], axis=0)
    shares = jnp.concatenate([shares, jnp.zeros_like(shares)], axis=1)
    columns = jnp.transpose(shares)
    for n in range(count):
        for head in range(kv_heads):
            rows = slice(head * size, (head + 1) * size)
            place = n * kv_heads + head
            share = columns[:size, place : place + 1]
            sum_ref[block_ref[n], rows, :] += share * parts[n][rows, :].astype(jnp.float32)
    row = lax.broadcasted_iota(jnp.int32, (tokens * blocks, tokens * blocks), 0)
    column = lax.broadcasted_iota(jnp.int32, (tokens * blocks, tokens * blocks), 1)
    turned = (row // blocks == column % tokens) & (row % blocks == column // tokens)
    turn = jnp.where(turned, 1.0, 0.0).astype(jnp.bfloat16)
    part = TILE * HEAD_DIM
    for head in range(kv_heads):
        lanes = []
        for g in range(TILE):
            first = head * size + g * tokens
            lanes.append(
                jnp.concatenate(
                    [sum_ref[b, first : first + tokens, :] for b in range(blocks)], axis=0
                )
            )
        block_rows = jnp.concatenate(lanes, axis=1).astype(jnp.bfloat16)
        token_rows = jnp.dot(turn, block_rows, preferred_element_type=jnp.float32)
        for t in range(tokens):
            out_ref[t, :, head * part : (head + 1) * part] = token_rows[
                t * blocks : (t + 1) * blocks
            ].astype(jnp.bfloat16)


def merge_pages(block_of, parts, like):
    count = len(parts)
    tokens, blocks, width = like.shape
    kv_heads = width // (TILE * HEAD_DIM)
    size = TILE * tokens
    return pl.pallas_call(
        functools.partial(merge_kernel, count),
        out_shape=jax.ShapeDtypeStruct(like.shape, jnp.bfloat16),
        in_specs=[pl.BlockSpec(memory_space=pltpu.SMEM)]
        + [pl.BlockSpec(memory_space=pltpu.VMEM)] * count,
        out_specs=pl.BlockSpec(memory_space=pltpu.VMEM),
        scratch_shapes=[
            pltpu.VMEM((blocks, kv_heads * size, HEAD_DIM), jnp.float32),
            pltpu.VMEM((blocks, kv_heads, size), jnp.float32),
            pltpu.VMEM((blocks, kv_heads, size), jnp.float32),
        ],
        compiler_params=pltpu.CompilerParams(vmem_limit_bytes=VMEM_BYTES),
        cost_estimate=pl.CostEstimate(flops=0, bytes_accessed=4 << 20, transcendentals=0),
        name="merge_pages",
    )(block_of, *parts)


class Window:
    def __init__(self, depth):
        self.depth, self.arrived = depth, []

    def swap(self, value, step):
        if step == 0:
            return value
        if len(self.arrived) >= self.depth:
            value, _ = lax.optimization_barrier((value, self.arrived[-self.depth]))
        count = lax.axis_size("ctx")
        pairs = [(source, source ^ step) for source in range(count)]
        self.arrived.append(lax.ppermute(value, "ctx", pairs))
        return self.arrived[-1]


def stepped_body(queries, kv_cache, page_counts, doc_ids):
    peers = lax.axis_size("ctx")
    pages = lax.axis_index("ctx") ^ jnp.arange(peers, dtype=jnp.int32)
    block_of = page_blocks(pages, page_counts, doc_ids)
    half = peers // 2
    window = Window(4)
    far = dict(zip(range(half, peers), pack_queries(queries, block_of[half:])))
    near = dict(zip(range(half), pack_queries(queries, block_of[:half])))
    sent = {**far, **near}
    asked, parts = {}, {}

    def ask(*steps):
        for step in steps:
            asked[step] = window.swap(sent[step], step)

    def attend(*steps):
        for step, part in zip(steps, attend_page(kv_cache[0], [asked[s] for s in steps])):
            parts[step] = part

    def answer(*steps):
        for step in steps:
            parts[step] = window.swap(parts[step], step)

    ask(8, 9, 1, 10, 11, 2, 4, 12, 13, 3, 14, 5, 15, 6, 7, 0)
    attend(0, 1, 2, 3)
    attend(8, 9, 10, 11)
    answer(8, 9, 1, 10, 2)
    attend(4, 5, 6, 7)
    answer(11, 4, 3)
    attend(12, 13, 14, 15)
    answer(12, 5, 13, 6, 14, 7, 15)
    return merge_pages(block_of, [parts[step] for step in range(peers)], queries)


def body(queries, kv_cache, page_counts, doc_ids):
    tokens, blocks, width = queries.shape
    groups = width // kv_cache.shape[-1]
    fits = tokens == TILE and blocks == TILE and groups == TILE and lax.axis_size("ctx") == 2 * TILE
    chosen = stepped_body if fits else gathered_body
    return chosen(queries, kv_cache, page_counts, doc_ids)


def solution(mesh):
    placed = (
        P(("group", "ctx"), None, None),
        P(("group", "ctx"), None, None, None),
        P("group"),
        P("group"),
    )
    return jax.shard_map(
        body, mesh=mesh, in_specs=placed, out_specs=P(("group", "ctx"), None, None), check_vma=False
    )
```

```python
import functools
import math

import jax
import jax.numpy as jnp
from jax import lax
from jax.experimental import pallas as pl
from jax.experimental.pallas import tpu as pltpu
from jax.sharding import PartitionSpec as P

HEAD_DIM = 128
TILE = 8
STAT_ROWS = 16
VMEM_BYTES = 32 * 1024 * 1024


def doc_of(pages, doc_ends):
    return jnp.sum((pages[..., None] >= doc_ends).astype(jnp.int32), axis=-1)


def page_partial(rows, page_kv):
    tokens = rows.shape[0]
    kv_heads = page_kv.shape[-1] // HEAD_DIM
    groups = rows.shape[-1] // (kv_heads * HEAD_DIM)
    grouped = rows.reshape(tokens, kv_heads, groups, HEAD_DIM)
    keys = page_kv[0].reshape(-1, kv_heads, HEAD_DIM)
    values = page_kv[1].reshape(-1, kv_heads, HEAD_DIM)
    scores = jnp.einsum(
        "qhgd,khd->qhgk", grouped, keys, preferred_element_type=jnp.float32
    ) * HEAD_DIM ** (-0.5)
    row_max = jnp.max(scores, axis=-1)
    expo = jnp.exp(scores - row_max[..., None])
    row_sum = jnp.sum(expo, axis=-1)
    weights = expo.astype(jnp.bfloat16)
    mixed = jnp.einsum("qhgk,khd->qhgd", weights, values, preferred_element_type=jnp.float32)
    return (row_max.reshape(tokens, -1), row_sum.reshape(tokens, -1), mixed.reshape(tokens, -1))


def page_blocks(pages, page_counts, doc_ids):
    block_order = jnp.arange(doc_ids.shape[0], dtype=jnp.int32)
    page_docs = doc_of(pages, jnp.cumsum(page_counts))
    return jnp.sum(jnp.where(doc_ids == page_docs[:, None], block_order, 0), axis=-1)


def gathered_body(queries, kv_cache, page_counts, doc_ids):
    peers = lax.axis_size("ctx")
    local_rows, blocks, width = queries.shape
    heads = width // HEAD_DIM
    block_of = page_blocks(jnp.arange(peers, dtype=jnp.int32), page_counts, doc_ids)
    outgoing = jnp.take(queries, block_of, axis=1)
    arrived = lax.all_to_all(outgoing, "ctx", split_axis=1, concat_axis=0, tiled=True)
    row_max, row_sum, mixed = page_partial(arrived.reshape(-1, width), kv_cache[0])
    send = [part.reshape(peers, local_rows, -1) for part in (mixed, row_max, row_sum)]
    got_out, got_max, got_sum = [
        lax.all_to_all(part, "ctx", split_axis=0, concat_axis=0, tiled=True) for part in send
    ]
    matches = (block_of == jnp.arange(blocks, dtype=jnp.int32)[:, None])[..., None, None]
    masked = jnp.where(matches, got_max, -1e30)
    row_top = jnp.max(masked, axis=1, keepdims=True)
    weight = jnp.where(matches, jnp.exp(masked - row_top), 0.0)
    denominator = jnp.sum(weight * got_sum, axis=1)
    numerator = jnp.einsum(
        "cnrh,nrhd->crhd",
        weight,
        got_out.reshape(peers, local_rows, heads, HEAD_DIM),
        precision=lax.Precision.HIGHEST,
    )
    mixed_out = (numerator / denominator[..., None]).reshape(blocks, local_rows, width)
    return jnp.moveaxis(mixed_out, 0, 1).astype(jnp.bfloat16)


def pack_kernel(count, counts_hbm, ids_hbm, query_ref, block_ref, *refs):
    sent_refs, (rows_ref, counts_ref, ids_ref, arrival, read) = refs[:count], refs[count:]
    small = [
        pltpu.make_async_copy(counts_hbm, counts_ref, read.at[0]),
        pltpu.make_async_copy(ids_hbm, ids_ref, read.at[1]),
    ]
    for copy in small:
        copy.start()
    tokens, blocks, width = query_ref.shape
    part = TILE * HEAD_DIM
    heads = range(width // part)
    spans = [slice(head * part, (head + 1) * part) for head in heads]
    copies = [
        pltpu.make_async_copy(query_ref.at[:, :, span], rows_ref.at[:, :, span], arrival.at[head])
        for head, span in zip(heads, spans)
    ]
    for copy in copies:
        copy.start()
    for copy in small:
        copy.wait()
    own = lax.axis_index("ctx")
    ends, end = [], 0
    for doc in range(blocks):
        end = end + counts_ref[doc]
        ends.append(end)
    ids = [ids_ref[block] for block in range(blocks)]
    asking = []
    for step in range(count):
        page = own ^ step
        doc = sum((page >= end).astype(jnp.int32) for end in ends)
        block = sum(jnp.where(ids[c] == doc, c, 0) for c in range(1, blocks))
        block_ref[step] = block
        asking.append(block)
    row = lax.broadcasted_iota(jnp.int32, (tokens, tokens * blocks), 0)
    column = lax.broadcasted_iota(jnp.int32, (tokens, tokens * blocks), 1)
    pick = jnp.concatenate(
        [jnp.where(column == row * blocks + block, 1.0, 0.0) for block in asking], axis=0
    ).astype(jnp.bfloat16)
    size = TILE * tokens
    for head in heads:
        copies[head].wait()
        rows = jnp.concatenate(
            [rows_ref[t, :, spans[head]].astype(jnp.float32) for t in range(tokens)], axis=0
        ).astype(jnp.bfloat16)
        picked = jnp.dot(pick, rows, preferred_element_type=jnp.float32)
        for n in range(count):
            own_rows = picked[n * tokens : (n + 1) * tokens]
            own_rows = jnp.concatenate(
                [own_rows[:, g * HEAD_DIM : (g + 1) * HEAD_DIM] for g in range(TILE)], axis=0
            )
            sent_refs[n][head * size : (head + 1) * size, :] = own_rows.astype(jnp.bfloat16)


def pack_queries(queries, page_counts, doc_ids):
    count = lax.axis_size("ctx")
    tokens, _, width = queries.shape
    rows = tokens * width // HEAD_DIM
    vmem, smem = pl.BlockSpec(memory_space=pltpu.VMEM), pl.BlockSpec(memory_space=pltpu.SMEM)
    hbm = pl.BlockSpec(memory_space=pltpu.HBM)
    block_of, *sent = pl.pallas_call(
        functools.partial(pack_kernel, count),
        out_shape=[jax.ShapeDtypeStruct((count,), jnp.int32)]
        + [jax.ShapeDtypeStruct((rows, HEAD_DIM), jnp.bfloat16)] * count,
        in_specs=[hbm, hbm, hbm],
        out_specs=[smem] + [vmem] * count,
        scratch_shapes=[
            pltpu.VMEM(queries.shape, jnp.bfloat16),
            pltpu.SMEM(page_counts.shape, jnp.int32),
            pltpu.SMEM(doc_ids.shape, jnp.int32),
            pltpu.SemaphoreType.DMA((width // (TILE * HEAD_DIM),)),
            pltpu.SemaphoreType.DMA((2,)),
        ],
        cost_estimate=pl.CostEstimate(flops=0, bytes_accessed=4 << 20, transcendentals=0),
        name="pack_queries",
    )(page_counts, doc_ids, queries)
    return block_of, sent


def attend_kernel(count, kv_ref, *refs):
    asked, answers, log_ref = refs[:count], refs[count : 2 * count], refs[2 * count]
    kv_heads = kv_ref.shape[2] // HEAD_DIM
    size = asked[0].shape[0] // kv_heads
    scale = HEAD_DIM ** (-0.5)

    for head in range(kv_heads):
        lanes = slice(head * HEAD_DIM, (head + 1) * HEAD_DIM)
        rows = slice(head * size, (head + 1) * size)
        query = jnp.concatenate([ref[rows, :] for ref in asked], axis=0)
        scores = lax.dot_general(
            kv_ref[0, :, lanes], query, (((1,), (1,)), ((), ())), preferred_element_type=jnp.float32
        )
        top = jnp.max(scores, axis=0, keepdims=True)
        expo = jnp.exp2((scores - top) * (scale / math.log(2.0)))
        total = jnp.sum(expo, axis=0, keepdims=True)
        mixed = lax.dot_general(
            expo.astype(jnp.bfloat16),
            kv_ref[1, :, lanes],
            (((0,), (0,)), ((), ())),
            preferred_element_type=jnp.float32,
        )
        mixed = mixed * jnp.transpose(jnp.broadcast_to(1.0 / total, (HEAD_DIM, total.shape[1])))
        for n in range(count):
            answers[n][rows, :] = mixed[n * size : (n + 1) * size].astype(jnp.bfloat16)
        log_ref[head : head + 1, :] = top * scale + jnp.log(total)
    logs = log_ref[...]
    high = logs.astype(jnp.bfloat16).astype(jnp.float32)
    middle = (logs - high).astype(jnp.bfloat16).astype(jnp.float32)
    low = logs - high - middle
    for n in range(count):
        span = slice(n * size, (n + 1) * size)
        upper = jnp.concatenate([high[:, span], middle[:, span]], axis=1)
        lower = jnp.concatenate([low[:, span], jnp.zeros_like(low[:, span])], axis=1)
        answers[n][kv_heads * size :, :] = jnp.concatenate([upper, lower], axis=0).astype(
            jnp.bfloat16
        )


def attend_page(page_kv, asked):
    count = len(asked)
    rows = asked[0].shape[0]
    kv_heads = page_kv.shape[2] // HEAD_DIM
    flops = 4 * count * rows * page_kv.shape[1] * HEAD_DIM
    return pl.pallas_call(
        functools.partial(attend_kernel, count),
        out_shape=[jax.ShapeDtypeStruct((rows + STAT_ROWS, HEAD_DIM), jnp.bfloat16)] * count,
        in_specs=[pl.BlockSpec(memory_space=pltpu.VMEM)] * (1 + count),
        out_specs=[pl.BlockSpec(memory_space=pltpu.VMEM)] * count,
        scratch_shapes=[pltpu.VMEM((kv_heads, count * rows // kv_heads), jnp.float32)],
        compiler_params=pltpu.CompilerParams(vmem_limit_bytes=VMEM_BYTES),
        cost_estimate=pl.CostEstimate(
            flops=flops, bytes_accessed=3 << 20, transcendentals=flops // 512
        ),
        name="attend_page",
    )(page_kv, *asked)


def merge_kernel(count, block_ref, *refs):
    parts, (out_ref, top_ref, total_ref, done_ref, leaving) = refs[:count], refs[count : count + 5]
    sum_refs = refs[count + 5 :]
    tokens, blocks, width = out_ref.shape
    size = TILE * tokens
    part = TILE * HEAD_DIM
    kv_heads = width // part
    top_ref[...] = jnp.full(top_ref.shape, -1e30, jnp.float32)
    total_ref[...] = jnp.zeros(total_ref.shape, jnp.float32)
    for sum_ref in sum_refs:
        sum_ref[...] = jnp.zeros(sum_ref.shape, jnp.float32)
    asking = [block_ref[n] for n in range(count)]
    logs = []
    for n in range(count):
        stat = parts[n][kv_heads * size :, :].astype(jnp.float32)
        log = stat[:kv_heads, :size] + stat[:kv_heads, size:] + stat[kv_heads:, :size]
        logs.append(log)
        top_ref[asking[n]] = jnp.maximum(top_ref[asking[n]], log)
    shares = [jnp.exp(logs[n] - top_ref[asking[n]]) for n in range(count)]
    for n in range(count):
        total_ref[asking[n]] += shares[n]
    shares = jnp.concatenate([shares[n] / total_ref[asking[n]] for n in range(count)], axis=0)
    shares = jnp.concatenate([shares, jnp.zeros_like(shares)], axis=1)
    columns = jnp.transpose(shares)
    row = lax.broadcasted_iota(jnp.int32, (tokens * blocks, tokens * blocks), 0)
    column = lax.broadcasted_iota(jnp.int32, (tokens * blocks, tokens * blocks), 1)
    turned = (row // blocks == column % tokens) & (row % blocks == column // tokens)
    turn = jnp.where(turned, 1.0, 0.0).astype(jnp.bfloat16)
    for n in range(count):
        for head, sum_ref in enumerate(sum_refs):
            place = n * kv_heads + head
            share = columns[:size, place : place + 1]
            part_rows = parts[n][head * size : (head + 1) * size, :]
            sum_ref[asking[n]] += share * part_rows.astype(jnp.float32)
    copies = []
    for head, sum_ref in enumerate(sum_refs):
        span = slice(head * part, (head + 1) * part)
        lanes = [
            jnp.concatenate(
                [sum_ref[b, g * tokens : (g + 1) * tokens, :] for b in range(blocks)], axis=0
            )
            for g in range(TILE)
        ]
        block_rows = jnp.concatenate(lanes, axis=1).astype(jnp.bfloat16)
        token_rows = jnp.dot(turn, block_rows, preferred_element_type=jnp.float32)
        for t in range(tokens):
            done_ref[t, :, span] = token_rows[t * blocks : (t + 1) * blocks].astype(jnp.bfloat16)
        copy = pltpu.make_async_copy(
            done_ref.at[:, :, span], out_ref.at[:, :, span], leaving.at[head]
        )
        copy.start()
        copies.append(copy)
    for copy in copies:
        copy.wait()


def merge_pages(block_of, parts, like):
    count = len(parts)
    tokens, blocks, width = like.shape
    kv_heads = width // (TILE * HEAD_DIM)
    size = TILE * tokens
    return pl.pallas_call(
        functools.partial(merge_kernel, count),
        out_shape=jax.ShapeDtypeStruct(like.shape, jnp.bfloat16),
        in_specs=[pl.BlockSpec(memory_space=pltpu.SMEM)]
        + [pl.BlockSpec(memory_space=pltpu.VMEM)] * count,
        out_specs=pl.BlockSpec(memory_space=pltpu.HBM),
        scratch_shapes=[
            pltpu.VMEM((blocks, kv_heads, size), jnp.float32),
            pltpu.VMEM((blocks, kv_heads, size), jnp.float32),
            pltpu.VMEM(like.shape, jnp.bfloat16),
            pltpu.SemaphoreType.DMA((kv_heads,)),
        ]
        + [pltpu.VMEM((blocks, size, HEAD_DIM), jnp.float32)] * kv_heads,
        compiler_params=pltpu.CompilerParams(vmem_limit_bytes=VMEM_BYTES),
        cost_estimate=pl.CostEstimate(flops=0, bytes_accessed=4 << 20, transcendentals=0),
        name="merge_pages",
    )(block_of, *parts)


class Window:
    def __init__(self, far, depth):
        self.far, self.depth = far, depth
        self.arrived = {False: [], True: []}

    def swap(self, value, step):
        if step == 0:
            return value
        arrived = self.arrived[step >= self.far]
        if len(arrived) >= self.depth:
            value, _ = lax.optimization_barrier((value, arrived[-self.depth]))
        count = lax.axis_size("ctx")
        pairs = [(source, source ^ step) for source in range(count)]
        arrived.append(lax.ppermute(value, "ctx", pairs))
        return arrived[-1]


def stepped_body(queries, kv_cache, page_counts, doc_ids):
    block_of, sent = pack_queries(queries, page_counts, doc_ids)
    window = Window(len(sent) // 2, 3)
    asked, parts = {}, {}

    def ask(*steps):
        for step in steps:
            asked[step] = window.swap(sent[step], step)

    def attend(*steps):
        for step, part in zip(steps, attend_page(kv_cache[0], [asked[s] for s in steps])):
            parts[step] = part

    def answer(*steps):
        for step in steps:
            parts[step] = window.swap(parts[step], step)

    ask(8, 9, 1, 10, 11, 2, 4, 12, 13, 3, 14, 5, 15, 6, 7, 0)
    attend(0, 1, 2, 3)
    attend(8, 9, 10, 11)
    answer(8, 9, 1, 10, 2)
    attend(4, 5, 6, 7)
    answer(11, 4, 3)
    attend(12, 13, 14, 15)
    answer(12, 5, 13, 6, 14, 7, 15)
    return merge_pages(block_of, [parts[step] for step in range(len(sent))], queries)


def body(queries, kv_cache, page_counts, doc_ids):
    tokens, blocks, width = queries.shape
    groups = width // kv_cache.shape[-1]
    fits = tokens == TILE and blocks == TILE and groups == TILE and lax.axis_size("ctx") == 2 * TILE
    chosen = stepped_body if fits else gathered_body
    return chosen(queries, kv_cache, page_counts, doc_ids)


def solution(mesh):
    placed = (
        P(("group", "ctx"), None, None),
        P(("group", "ctx"), None, None, None),
        P("group"),
        P("group"),
    )
    return jax.shard_map(
        body, mesh=mesh, in_specs=placed, out_specs=P(("group", "ctx"), None, None), check_vma=False
    )
```

```python
import functools
import math

import jax
import jax.numpy as jnp
from jax import lax
from jax.experimental import pallas as pl
from jax.experimental.pallas import tpu as pltpu
from jax.sharding import PartitionSpec as P

HEAD_DIM = 128
TILE = 8
STAT_ROWS = 16
VMEM_BYTES = 32 * 1024 * 1024


def doc_of(pages, doc_ends):
    return jnp.sum((pages[..., None] >= doc_ends).astype(jnp.int32), axis=-1)


def page_partial(rows, page_kv):
    tokens = rows.shape[0]
    kv_heads = page_kv.shape[-1] // HEAD_DIM
    groups = rows.shape[-1] // (kv_heads * HEAD_DIM)
    grouped = rows.reshape(tokens, kv_heads, groups, HEAD_DIM)
    keys = page_kv[0].reshape(-1, kv_heads, HEAD_DIM)
    values = page_kv[1].reshape(-1, kv_heads, HEAD_DIM)
    scores = jnp.einsum(
        "qhgd,khd->qhgk", grouped, keys, preferred_element_type=jnp.float32
    ) * HEAD_DIM ** (-0.5)
    row_max = jnp.max(scores, axis=-1)
    expo = jnp.exp(scores - row_max[..., None])
    row_sum = jnp.sum(expo, axis=-1)
    weights = expo.astype(jnp.bfloat16)
    mixed = jnp.einsum("qhgk,khd->qhgd", weights, values, preferred_element_type=jnp.float32)
    return (row_max.reshape(tokens, -1), row_sum.reshape(tokens, -1), mixed.reshape(tokens, -1))


def page_blocks(pages, page_counts, doc_ids):
    block_order = jnp.arange(doc_ids.shape[0], dtype=jnp.int32)
    page_docs = doc_of(pages, jnp.cumsum(page_counts))
    return jnp.sum(jnp.where(doc_ids == page_docs[:, None], block_order, 0), axis=-1)


def gathered_body(queries, kv_cache, page_counts, doc_ids):
    peers = lax.axis_size("ctx")
    local_rows, blocks, width = queries.shape
    heads = width // HEAD_DIM
    block_of = page_blocks(jnp.arange(peers, dtype=jnp.int32), page_counts, doc_ids)
    outgoing = jnp.take(queries, block_of, axis=1)
    arrived = lax.all_to_all(outgoing, "ctx", split_axis=1, concat_axis=0, tiled=True)
    row_max, row_sum, mixed = page_partial(arrived.reshape(-1, width), kv_cache[0])
    send = [part.reshape(peers, local_rows, -1) for part in (mixed, row_max, row_sum)]
    got_out, got_max, got_sum = [
        lax.all_to_all(part, "ctx", split_axis=0, concat_axis=0, tiled=True) for part in send
    ]
    matches = (block_of == jnp.arange(blocks, dtype=jnp.int32)[:, None])[..., None, None]
    masked = jnp.where(matches, got_max, -1e30)
    row_top = jnp.max(masked, axis=1, keepdims=True)
    weight = jnp.where(matches, jnp.exp(masked - row_top), 0.0)
    denominator = jnp.sum(weight * got_sum, axis=1)
    numerator = jnp.einsum(
        "cnrh,nrhd->crhd",
        weight,
        got_out.reshape(peers, local_rows, heads, HEAD_DIM),
        precision=lax.Precision.HIGHEST,
    )
    mixed_out = (numerator / denominator[..., None]).reshape(blocks, local_rows, width)
    return jnp.moveaxis(mixed_out, 0, 1).astype(jnp.bfloat16)


def pack_kernel(steps, listed, counts_hbm, ids_hbm, query_ref, block_ref, *refs):
    count = len(steps)
    sent_refs, (rows_ref, counts_ref, ids_ref, arrival, read) = refs[:count], refs[count:]
    small = [
        pltpu.make_async_copy(counts_hbm, counts_ref, read.at[0]),
        pltpu.make_async_copy(ids_hbm, ids_ref, read.at[1]),
    ]
    for copy in small:
        copy.start()
    tokens, blocks, width = query_ref.shape
    part = TILE * HEAD_DIM
    heads = range(width // part)
    spans = [slice(head * part, (head + 1) * part) for head in heads]
    copies = [
        pltpu.make_async_copy(query_ref.at[:, :, span], rows_ref.at[:, :, span], arrival.at[head])
        for head, span in zip(heads, spans)
    ]
    for copy in copies:
        copy.start()
    for copy in small:
        copy.wait()
    own = lax.axis_index("ctx")
    ends, end = [], 0
    for doc in range(blocks):
        end = end + counts_ref[doc]
        ends.append(end)
    ids = [ids_ref[block] for block in range(blocks)]
    asking = {}
    for n, step in enumerate(listed):
        page = own ^ step
        doc = sum((page >= end).astype(jnp.int32) for end in ends)
        block = sum(jnp.where(ids[c] == doc, c, 0) for c in range(1, blocks))
        block_ref[n] = block
        asking[step] = block
    row = lax.broadcasted_iota(jnp.int32, (tokens, tokens * blocks), 0)
    column = lax.broadcasted_iota(jnp.int32, (tokens, tokens * blocks), 1)
    pick = jnp.concatenate(
        [jnp.where(column == row * blocks + asking[step], 1.0, 0.0) for step in steps], axis=0
    ).astype(jnp.bfloat16)
    size = TILE * tokens
    for head in heads:
        copies[head].wait()
        rows = jnp.concatenate(
            [rows_ref[t, :, spans[head]].astype(jnp.float32) for t in range(tokens)], axis=0
        ).astype(jnp.bfloat16)
        picked = jnp.dot(pick, rows, preferred_element_type=jnp.float32)
        for n in range(count):
            own_rows = picked[n * tokens : (n + 1) * tokens]
            own_rows = jnp.concatenate(
                [own_rows[:, g * HEAD_DIM : (g + 1) * HEAD_DIM] for g in range(TILE)], axis=0
            )
            sent_refs[n][head * size : (head + 1) * size, :] = own_rows.astype(jnp.bfloat16)


def pack_queries(queries, page_counts, doc_ids, steps, listed):
    count = len(steps)
    tokens, _, width = queries.shape
    rows = tokens * width // HEAD_DIM
    vmem, smem = pl.BlockSpec(memory_space=pltpu.VMEM), pl.BlockSpec(memory_space=pltpu.SMEM)
    hbm = pl.BlockSpec(memory_space=pltpu.HBM)
    block_of, *sent = pl.pallas_call(
        functools.partial(pack_kernel, steps, listed),
        out_shape=[jax.ShapeDtypeStruct((len(listed),), jnp.int32)]
        + [jax.ShapeDtypeStruct((rows, HEAD_DIM), jnp.bfloat16)] * count,
        in_specs=[hbm, hbm, hbm],
        out_specs=[smem] + [vmem] * count,
        scratch_shapes=[
            pltpu.VMEM(queries.shape, jnp.bfloat16),
            pltpu.SMEM(page_counts.shape, jnp.int32),
            pltpu.SMEM(doc_ids.shape, jnp.int32),
            pltpu.SemaphoreType.DMA((width // (TILE * HEAD_DIM),)),
            pltpu.SemaphoreType.DMA((2,)),
        ],
        cost_estimate=pl.CostEstimate(flops=0, bytes_accessed=4 << 20, transcendentals=0),
        name="pack_queries",
    )(page_counts, doc_ids, queries)
    return block_of, sent


def attend_kernel(count, kv_ref, *refs):
    asked, answers, log_ref = refs[:count], refs[count : 2 * count], refs[2 * count]
    kv_heads = kv_ref.shape[2] // HEAD_DIM
    size = asked[0].shape[0] // kv_heads
    scale = HEAD_DIM ** (-0.5)

    for head in range(kv_heads):
        lanes = slice(head * HEAD_DIM, (head + 1) * HEAD_DIM)
        rows = slice(head * size, (head + 1) * size)
        query = jnp.concatenate([ref[rows, :] for ref in asked], axis=0)
        scores = lax.dot_general(
            kv_ref[0, :, lanes], query, (((1,), (1,)), ((), ())), preferred_element_type=jnp.float32
        )
        top = jnp.max(scores, axis=0, keepdims=True)
        expo = jnp.exp2((scores - top) * (scale / math.log(2.0)))
        total = jnp.sum(expo, axis=0, keepdims=True)
        mixed = lax.dot_general(
            expo.astype(jnp.bfloat16),
            kv_ref[1, :, lanes],
            (((0,), (0,)), ((), ())),
            preferred_element_type=jnp.float32,
        )
        mixed = mixed * jnp.transpose(jnp.broadcast_to(1.0 / total, (HEAD_DIM, total.shape[1])))
        for n in range(count):
            answers[n][rows, :] = mixed[n * size : (n + 1) * size].astype(jnp.bfloat16)
        log_ref[head : head + 1, :] = top * scale + jnp.log(total)
    logs = log_ref[...]
    high = logs.astype(jnp.bfloat16).astype(jnp.float32)
    middle = (logs - high).astype(jnp.bfloat16).astype(jnp.float32)
    low = logs - high - middle
    for n in range(count):
        span = slice(n * size, (n + 1) * size)
        upper = jnp.concatenate([high[:, span], middle[:, span]], axis=1)
        lower = jnp.concatenate([low[:, span], jnp.zeros_like(low[:, span])], axis=1)
        answers[n][kv_heads * size :, :] = jnp.concatenate([upper, lower], axis=0).astype(
            jnp.bfloat16
        )


def attend_page(page_kv, asked):
    count = len(asked)
    rows = asked[0].shape[0]
    kv_heads = page_kv.shape[2] // HEAD_DIM
    flops = 4 * count * rows * page_kv.shape[1] * HEAD_DIM
    return pl.pallas_call(
        functools.partial(attend_kernel, count),
        out_shape=[jax.ShapeDtypeStruct((rows + STAT_ROWS, HEAD_DIM), jnp.bfloat16)] * count,
        in_specs=[pl.BlockSpec(memory_space=pltpu.VMEM)] * (1 + count),
        out_specs=[pl.BlockSpec(memory_space=pltpu.VMEM)] * count,
        scratch_shapes=[pltpu.VMEM((kv_heads, count * rows // kv_heads), jnp.float32)],
        compiler_params=pltpu.CompilerParams(vmem_limit_bytes=VMEM_BYTES),
        cost_estimate=pl.CostEstimate(
            flops=flops, bytes_accessed=3 << 20, transcendentals=flops // 512
        ),
        name="attend_page",
    )(page_kv, *asked)


def unpack_logs(part_ref, kv_heads):
    stat = part_ref[part_ref.shape[0] - STAT_ROWS :, :].astype(jnp.float32)
    size = stat.shape[1] // 2
    return stat[:kv_heads, :size] + stat[:kv_heads, size:] + stat[kv_heads:, :size]


def as_columns(shares):
    rows = jnp.concatenate(shares, axis=0)
    rows = jnp.concatenate([rows, jnp.zeros_like(rows)], axis=1)
    missing = HEAD_DIM - rows.shape[0] % HEAD_DIM
    if missing < HEAD_DIM:
        rows = jnp.concatenate([rows, jnp.zeros((missing, rows.shape[1]), jnp.float32)], axis=0)
    return jnp.transpose(rows)


def merge_kernel(steps, block_ref, *refs):
    count = len(steps)
    parts, (base_ref, top_ref, total_ref) = refs[:count], refs[count : count + 3]
    sum_refs = refs[count + 3 :]
    tokens, blocks, width = base_ref.shape
    size = TILE * tokens
    part = TILE * HEAD_DIM
    kv_heads = width // part
    top_ref[...] = jnp.full(top_ref.shape, -1e30, jnp.float32)
    total_ref[...] = jnp.zeros(total_ref.shape, jnp.float32)
    for sum_ref in sum_refs:
        sum_ref[...] = jnp.zeros(sum_ref.shape, jnp.float32)
    asking = [block_ref[step] for step in steps]
    logs = [unpack_logs(parts[n], kv_heads) for n in range(count)]
    for n in range(count):
        top_ref[asking[n]] = jnp.maximum(top_ref[asking[n]], logs[n])
    shares = [jnp.exp(logs[n] - top_ref[asking[n]]) for n in range(count)]
    for n in range(count):
        total_ref[asking[n]] += shares[n]
    columns = as_columns([shares[n] / total_ref[asking[n]] for n in range(count)])
    for n in range(count):
        for head, sum_ref in enumerate(sum_refs):
            place = n * kv_heads + head
            share = columns[:size, place : place + 1]
            part_rows = parts[n][head * size : (head + 1) * size, :]
            sum_ref[asking[n]] += share * part_rows.astype(jnp.float32)
    row = lax.broadcasted_iota(jnp.int32, (tokens * blocks, tokens * blocks), 0)
    column = lax.broadcasted_iota(jnp.int32, (tokens * blocks, tokens * blocks), 1)
    turned = (row // blocks == column % tokens) & (row % blocks == column // tokens)
    turn = jnp.where(turned, 1.0, 0.0).astype(jnp.bfloat16)
    for head, sum_ref in enumerate(sum_refs):
        span = slice(head * part, (head + 1) * part)
        lanes = [
            jnp.concatenate(
                [sum_ref[b, g * tokens : (g + 1) * tokens, :] for b in range(blocks)], axis=0
            )
            for g in range(TILE)
        ]
        block_rows = jnp.concatenate(lanes, axis=1).astype(jnp.bfloat16)
        token_rows = jnp.dot(turn, block_rows, preferred_element_type=jnp.float32)
        for t in range(tokens):
            base_ref[t, :, span] = token_rows[t * blocks : (t + 1) * blocks].astype(jnp.bfloat16)


def merge_pages(block_of, steps, parts, like):
    count = len(steps)
    tokens, blocks, width = like.shape
    kv_heads = width // (TILE * HEAD_DIM)
    size = TILE * tokens
    vmem = pl.BlockSpec(memory_space=pltpu.VMEM)
    stats = jax.ShapeDtypeStruct((blocks, kv_heads, size), jnp.float32)
    sums = jax.ShapeDtypeStruct((blocks, size, HEAD_DIM), jnp.float32)
    return pl.pallas_call(
        functools.partial(merge_kernel, steps),
        out_shape=[jax.ShapeDtypeStruct(like.shape, jnp.bfloat16), stats, stats]
        + [sums] * kv_heads,
        in_specs=[pl.BlockSpec(memory_space=pltpu.SMEM)] + [vmem] * count,
        out_specs=[vmem] * (3 + kv_heads),
        compiler_params=pltpu.CompilerParams(vmem_limit_bytes=VMEM_BYTES),
        cost_estimate=pl.CostEstimate(flops=0, bytes_accessed=4 << 20, transcendentals=0),
        name="merge_pages",
    )(block_of, *[parts[step] for step in steps])


def settle_kernel(steps, block_ref, base_ref, top_ref, total_ref, *refs):
    count = len(steps)
    parts, sum_refs = refs[:count], refs[count:-3]
    out_ref, done_ref, leaving = refs[-3:]
    tokens, blocks, width = out_ref.shape
    size = TILE * tokens
    part = TILE * HEAD_DIM
    kv_heads = width // part
    asking = [block_ref[step] for step in steps]
    logs = [unpack_logs(ref, kv_heads) for ref in parts]
    shares = []
    for block in asking:
        old = top_ref[block]
        own = [jnp.where(asking[n] == block, logs[n], -1e30) for n in range(count)]
        top = functools.reduce(jnp.maximum, own, old)
        weights = [jnp.exp(old - top) * total_ref[block]] + [jnp.exp(log - top) for log in own]
        total = sum(weights)
        shares += [weight / total for weight in weights]
    columns = as_columns(shares)
    row = lax.broadcasted_iota(jnp.int32, (tokens * blocks, count * tokens), 0)
    column = lax.broadcasted_iota(jnp.int32, (tokens * blocks, count * tokens), 1)
    turned = jnp.zeros(row.shape, jnp.bool_)
    block_row = lax.broadcasted_iota(jnp.int32, (blocks, part), 0)
    fresh = jnp.zeros((blocks, part), jnp.bool_)
    for n, block in enumerate(asking):
        first = jnp.bool_(True)
        for m in range(n):
            first = first & (asking[m] != block)
        wanted = jnp.where(first, block, -1)
        turned = turned | (
            (row // blocks == column - n * tokens) & (row % blocks == wanted)
        )
        fresh = fresh | (block_row == block)
    turn = jnp.where(turned, 1.0, 0.0).astype(jnp.bfloat16)
    copies = []
    for head, sum_ref in enumerate(sum_refs):
        span = slice(head * part, (head + 1) * part)
        merged = []
        for n, block in enumerate(asking):
            rows = [sum_ref[block]]
            rows += [ref[head * size : (head + 1) * size, :].astype(jnp.float32) for ref in parts]
            total = None
            for m, value in enumerate(rows):
                place = (n * (count + 1) + m) * kv_heads + head
                term = columns[:size, place : place + 1] * value
                total = term if total is None else total + term
            merged.append(total)
        lanes = [
            jnp.concatenate([rows[g * tokens : (g + 1) * tokens, :] for rows in merged], axis=0)
            for g in range(TILE)
        ]
        block_rows = jnp.concatenate(lanes, axis=1).astype(jnp.bfloat16)
        token_rows = jnp.dot(turn, block_rows, preferred_element_type=jnp.float32)
        for t in range(tokens):
            new = token_rows[t * blocks : (t + 1) * blocks]
            old = base_ref[t, :, span].astype(jnp.float32)
            done_ref[t, :, span] = jnp.where(fresh, new, old).astype(jnp.bfloat16)
        copy = pltpu.make_async_copy(
            done_ref.at[:, :, span], out_ref.at[:, :, span], leaving.at[head]
        )
        copy.start()
        copies.append(copy)
    for copy in copies:
        copy.wait()


def settle_pages(block_of, merged, steps, parts):
    count = len(steps)
    base, top, total, *sums = merged
    vmem = pl.BlockSpec(memory_space=pltpu.VMEM)
    return pl.pallas_call(
        functools.partial(settle_kernel, steps),
        out_shape=jax.ShapeDtypeStruct(base.shape, jnp.bfloat16),
        in_specs=[pl.BlockSpec(memory_space=pltpu.SMEM)] + [vmem] * (3 + count + len(sums)),
        out_specs=pl.BlockSpec(memory_space=pltpu.HBM),
        scratch_shapes=[
            pltpu.VMEM(base.shape, jnp.bfloat16),
            pltpu.SemaphoreType.DMA((len(sums),)),
        ],
        compiler_params=pltpu.CompilerParams(vmem_limit_bytes=VMEM_BYTES),
        cost_estimate=pl.CostEstimate(flops=0, bytes_accessed=4 << 20, transcendentals=0),
        name="settle_pages",
    )(block_of, base, top, total, *[parts[step] for step in steps], *sums)


class Window:
    def __init__(self, far, depth):
        self.far, self.depth = far, depth
        self.arrived = {False: [], True: []}

    def swap(self, value, step):
        if step == 0:
            return value
        arrived = self.arrived[step >= self.far]
        if len(arrived) >= self.depth:
            value, _ = lax.optimization_barrier((value, arrived[-self.depth]))
        count = lax.axis_size("ctx")
        pairs = [(source, source ^ step) for source in range(count)]
        arrived.append(lax.ppermute(value, "ctx", pairs))
        return arrived[-1]


def stepped_body(queries, kv_cache, page_counts, doc_ids):
    every = tuple(range(lax.axis_size("ctx")))
    early = (8, 9, 1, 10)
    late = tuple(step for step in every if step not in early)
    _, first = pack_queries(queries, page_counts, doc_ids, early, early)
    block_of, rest = pack_queries(queries, page_counts, doc_ids, late, every)
    sent = dict(zip(early + late, first + rest))
    window = Window(len(every) // 2, 3)
    asked, parts = {}, {}

    def ask(*steps):
        for step in steps:
            asked[step] = window.swap(sent[step], step)

    def attend(*steps):
        for step, part in zip(steps, attend_page(kv_cache[0], [asked[s] for s in steps])):
            parts[step] = part

    def answer(*steps):
        for step in steps:
            parts[step] = window.swap(parts[step], step)

    ask(8, 9, 1, 10, 11, 2, 4, 12, 13, 3, 14, 5, 15, 6, 7, 0)
    attend(0, 1, 2, 3)
    attend(8, 9, 10, 11)
    answer(8, 9, 1, 10, 2)
    attend(4, 5, 6, 7)
    answer(11, 4, 3)
    attend(12, 13, 14, 15)
    answer(12, 5, 13, 6, 14, 7, 15)
    last = (7, 15)
    before = tuple(step for step in every if step not in last)
    merged = merge_pages(block_of, before, parts, queries)
    return settle_pages(block_of, merged, last, parts)


def body(queries, kv_cache, page_counts, doc_ids):
    tokens, blocks, width = queries.shape
    groups = width // kv_cache.shape[-1]
    fits = tokens == TILE and blocks == TILE and groups == TILE and lax.axis_size("ctx") == 2 * TILE
    chosen = stepped_body if fits else gathered_body
    return chosen(queries, kv_cache, page_counts, doc_ids)


def solution(mesh):
    placed = (
        P(("group", "ctx"), None, None),
        P(("group", "ctx"), None, None, None),
        P("group"),
        P("group"),
    )
    return jax.shard_map(
        body, mesh=mesh, in_specs=placed, out_specs=P(("group", "ctx"), None, None), check_vma=False
    )
```

```python
import functools
import math

import jax
import jax.numpy as jnp
from jax import lax
from jax.experimental import pallas as pl
from jax.experimental.pallas import tpu as pltpu
from jax.sharding import PartitionSpec as P

HEAD_DIM = 128
TILE = 8
STAT_ROWS = 16
VMEM_BYTES = 32 * 1024 * 1024


def doc_of(pages, doc_ends):
    return jnp.sum((pages[..., None] >= doc_ends).astype(jnp.int32), axis=-1)


def page_partial(rows, page_kv):
    tokens = rows.shape[0]
    kv_heads = page_kv.shape[-1] // HEAD_DIM
    groups = rows.shape[-1] // (kv_heads * HEAD_DIM)
    grouped = rows.reshape(tokens, kv_heads, groups, HEAD_DIM)
    keys = page_kv[0].reshape(-1, kv_heads, HEAD_DIM)
    values = page_kv[1].reshape(-1, kv_heads, HEAD_DIM)
    scores = jnp.einsum(
        "qhgd,khd->qhgk", grouped, keys, preferred_element_type=jnp.float32
    ) * HEAD_DIM ** (-0.5)
    row_max = jnp.max(scores, axis=-1)
    expo = jnp.exp(scores - row_max[..., None])
    row_sum = jnp.sum(expo, axis=-1)
    weights = expo.astype(jnp.bfloat16)
    mixed = jnp.einsum("qhgk,khd->qhgd", weights, values, preferred_element_type=jnp.float32)
    return (row_max.reshape(tokens, -1), row_sum.reshape(tokens, -1), mixed.reshape(tokens, -1))


def page_blocks(pages, page_counts, doc_ids):
    block_order = jnp.arange(doc_ids.shape[0], dtype=jnp.int32)
    page_docs = doc_of(pages, jnp.cumsum(page_counts))
    return jnp.sum(jnp.where(doc_ids == page_docs[:, None], block_order, 0), axis=-1)


def gathered_body(queries, kv_cache, page_counts, doc_ids):
    peers = lax.axis_size("ctx")
    local_rows, blocks, width = queries.shape
    heads = width // HEAD_DIM
    block_of = page_blocks(jnp.arange(peers, dtype=jnp.int32), page_counts, doc_ids)
    outgoing = jnp.take(queries, block_of, axis=1)
    arrived = lax.all_to_all(outgoing, "ctx", split_axis=1, concat_axis=0, tiled=True)
    row_max, row_sum, mixed = page_partial(arrived.reshape(-1, width), kv_cache[0])
    send = [part.reshape(peers, local_rows, -1) for part in (mixed, row_max, row_sum)]
    got_out, got_max, got_sum = [
        lax.all_to_all(part, "ctx", split_axis=0, concat_axis=0, tiled=True) for part in send
    ]
    matches = (block_of == jnp.arange(blocks, dtype=jnp.int32)[:, None])[..., None, None]
    masked = jnp.where(matches, got_max, -1e30)
    row_top = jnp.max(masked, axis=1, keepdims=True)
    weight = jnp.where(matches, jnp.exp(masked - row_top), 0.0)
    denominator = jnp.sum(weight * got_sum, axis=1)
    numerator = jnp.einsum(
        "cnrh,nrhd->crhd",
        weight,
        got_out.reshape(peers, local_rows, heads, HEAD_DIM),
        precision=lax.Precision.HIGHEST,
    )
    mixed_out = (numerator / denominator[..., None]).reshape(blocks, local_rows, width)
    return jnp.moveaxis(mixed_out, 0, 1).astype(jnp.bfloat16)


def pack_kernel(steps, listed, counts_hbm, ids_hbm, query_ref, block_ref, *refs):
    count = len(steps)
    sent_refs, (rows_ref, counts_ref, ids_ref, arrival, read) = refs[:count], refs[count:]
    small = [
        pltpu.make_async_copy(counts_hbm, counts_ref, read.at[0]),
        pltpu.make_async_copy(ids_hbm, ids_ref, read.at[1]),
    ]
    for copy in small:
        copy.start()
    tokens, blocks, width = query_ref.shape
    part = TILE * HEAD_DIM
    heads = range(width // part)
    spans = [slice(head * part, (head + 1) * part) for head in heads]
    copies = [
        pltpu.make_async_copy(query_ref.at[:, :, span], rows_ref.at[:, :, span], arrival.at[head])
        for head, span in zip(heads, spans)
    ]
    for copy in copies:
        copy.start()
    for copy in small:
        copy.wait()
    own = lax.axis_index("ctx")
    ends, end = [], 0
    for doc in range(blocks):
        end = end + counts_ref[doc]
        ends.append(end)
    ids = [ids_ref[block] for block in range(blocks)]
    asking = {}
    for n, step in enumerate(listed):
        page = own ^ step
        doc = sum((page >= end).astype(jnp.int32) for end in ends)
        block = sum(jnp.where(ids[c] == doc, c, 0) for c in range(1, blocks))
        block_ref[n] = block
        asking[step] = block
    row = lax.broadcasted_iota(jnp.int32, (tokens, tokens * blocks), 0)
    column = lax.broadcasted_iota(jnp.int32, (tokens, tokens * blocks), 1)
    pick = jnp.concatenate(
        [jnp.where(column == row * blocks + asking[step], 1.0, 0.0) for step in steps], axis=0
    ).astype(jnp.bfloat16)
    size = TILE * tokens
    for head in heads:
        copies[head].wait()
        rows = jnp.concatenate(
            [rows_ref[t, :, spans[head]].astype(jnp.float32) for t in range(tokens)], axis=0
        ).astype(jnp.bfloat16)
        picked = jnp.dot(pick, rows, preferred_element_type=jnp.float32)
        for n in range(count):
            own_rows = picked[n * tokens : (n + 1) * tokens]
            own_rows = jnp.concatenate(
                [own_rows[:, g * HEAD_DIM : (g + 1) * HEAD_DIM] for g in range(TILE)], axis=0
            )
            sent_refs[n][head * size : (head + 1) * size, :] = own_rows.astype(jnp.bfloat16)


def pack_queries(queries, page_counts, doc_ids, steps, listed):
    count = len(steps)
    tokens, _, width = queries.shape
    rows = tokens * width // HEAD_DIM
    vmem, smem = pl.BlockSpec(memory_space=pltpu.VMEM), pl.BlockSpec(memory_space=pltpu.SMEM)
    hbm = pl.BlockSpec(memory_space=pltpu.HBM)
    block_of, *sent = pl.pallas_call(
        functools.partial(pack_kernel, steps, listed),
        out_shape=[jax.ShapeDtypeStruct((len(listed),), jnp.int32)]
        + [jax.ShapeDtypeStruct((rows, HEAD_DIM), jnp.bfloat16)] * count,
        in_specs=[hbm, hbm, hbm],
        out_specs=[smem] + [vmem] * count,
        scratch_shapes=[
            pltpu.VMEM(queries.shape, jnp.bfloat16),
            pltpu.SMEM(page_counts.shape, jnp.int32),
            pltpu.SMEM(doc_ids.shape, jnp.int32),
            pltpu.SemaphoreType.DMA((width // (TILE * HEAD_DIM),)),
            pltpu.SemaphoreType.DMA((2,)),
        ],
        cost_estimate=pl.CostEstimate(flops=0, bytes_accessed=4 << 20, transcendentals=0),
        name="pack_queries",
    )(page_counts, doc_ids, queries)
    return block_of, sent


def attend_kernel(count, kv_ref, *refs):
    asked, answers, log_ref = refs[:count], refs[count : 2 * count], refs[2 * count]
    kv_heads = kv_ref.shape[2] // HEAD_DIM
    size = asked[0].shape[0] // kv_heads
    scale = HEAD_DIM ** (-0.5)

    for head in range(kv_heads):
        lanes = slice(head * HEAD_DIM, (head + 1) * HEAD_DIM)
        rows = slice(head * size, (head + 1) * size)
        query = jnp.concatenate([ref[rows, :] for ref in asked], axis=0)
        scores = lax.dot_general(
            kv_ref[0, :, lanes], query, (((1,), (1,)), ((), ())), preferred_element_type=jnp.float32
        )
        top = jnp.max(scores, axis=0, keepdims=True)
        expo = jnp.exp2((scores - top) * (scale / math.log(2.0)))
        total = jnp.sum(expo, axis=0, keepdims=True)
        mixed = lax.dot_general(
            expo.astype(jnp.bfloat16),
            kv_ref[1, :, lanes],
            (((0,), (0,)), ((), ())),
            preferred_element_type=jnp.float32,
        )
        mixed = mixed * jnp.transpose(jnp.broadcast_to(1.0 / total, (HEAD_DIM, total.shape[1])))
        for n in range(count):
            answers[n][rows, :] = mixed[n * size : (n + 1) * size].astype(jnp.bfloat16)
        log_ref[head : head + 1, :] = top * scale + jnp.log(total)
    logs = log_ref[...]
    high = logs.astype(jnp.bfloat16).astype(jnp.float32)
    middle = (logs - high).astype(jnp.bfloat16).astype(jnp.float32)
    low = logs - high - middle
    for n in range(count):
        span = slice(n * size, (n + 1) * size)
        upper = jnp.concatenate([high[:, span], middle[:, span]], axis=1)
        lower = jnp.concatenate([low[:, span], jnp.zeros_like(low[:, span])], axis=1)
        answers[n][kv_heads * size :, :] = jnp.concatenate([upper, lower], axis=0).astype(
            jnp.bfloat16
        )


def attend_page(page_kv, asked):
    count = len(asked)
    rows = asked[0].shape[0]
    kv_heads = page_kv.shape[2] // HEAD_DIM
    flops = 4 * count * rows * page_kv.shape[1] * HEAD_DIM
    return pl.pallas_call(
        functools.partial(attend_kernel, count),
        out_shape=[jax.ShapeDtypeStruct((rows + STAT_ROWS, HEAD_DIM), jnp.bfloat16)] * count,
        in_specs=[pl.BlockSpec(memory_space=pltpu.VMEM)] * (1 + count),
        out_specs=[pl.BlockSpec(memory_space=pltpu.VMEM)] * count,
        scratch_shapes=[pltpu.VMEM((kv_heads, count * rows // kv_heads), jnp.float32)],
        compiler_params=pltpu.CompilerParams(vmem_limit_bytes=VMEM_BYTES),
        cost_estimate=pl.CostEstimate(
            flops=flops, bytes_accessed=3 << 20, transcendentals=flops // 512
        ),
        name="attend_page",
    )(page_kv, *asked)


def unpack_logs(part_ref, kv_heads):
    stat = part_ref[part_ref.shape[0] - STAT_ROWS :, :].astype(jnp.float32)
    size = stat.shape[1] // 2
    return stat[:kv_heads, :size] + stat[:kv_heads, size:] + stat[kv_heads:, :size]


def as_columns(shares):
    rows = jnp.concatenate(shares, axis=0)
    rows = jnp.concatenate([rows, jnp.zeros_like(rows)], axis=1)
    missing = HEAD_DIM - rows.shape[0] % HEAD_DIM
    if missing < HEAD_DIM:
        rows = jnp.concatenate([rows, jnp.zeros((missing, rows.shape[1]), jnp.float32)], axis=0)
    return jnp.transpose(rows)


def merge_kernel(steps, block_ref, *refs):
    count = len(steps)
    parts, (base_ref, top_ref, total_ref) = refs[:count], refs[count : count + 3]
    sum_refs = refs[count + 3 :]
    tokens, blocks, width = base_ref.shape
    size = TILE * tokens
    part = TILE * HEAD_DIM
    kv_heads = width // part
    top_ref[...] = jnp.full(top_ref.shape, -1e30, jnp.float32)
    total_ref[...] = jnp.zeros(total_ref.shape, jnp.float32)
    for sum_ref in sum_refs:
        sum_ref[...] = jnp.zeros(sum_ref.shape, jnp.float32)
    asking = [block_ref[step] for step in steps]
    logs = [unpack_logs(parts[n], kv_heads) for n in range(count)]
    for n in range(count):
        top_ref[asking[n]] = jnp.maximum(top_ref[asking[n]], logs[n])
    shares = [jnp.exp(logs[n] - top_ref[asking[n]]) for n in range(count)]
    for n in range(count):
        total_ref[asking[n]] += shares[n]
    columns = as_columns([shares[n] / total_ref[asking[n]] for n in range(count)])
    for n in range(count):
        for head, sum_ref in enumerate(sum_refs):
            place = n * kv_heads + head
            share = columns[:size, place : place + 1]
            part_rows = parts[n][head * size : (head + 1) * size, :]
            sum_ref[asking[n]] += share * part_rows.astype(jnp.float32)
    row = lax.broadcasted_iota(jnp.int32, (tokens * blocks, tokens * blocks), 0)
    column = lax.broadcasted_iota(jnp.int32, (tokens * blocks, tokens * blocks), 1)
    turned = (row // blocks == column % tokens) & (row % blocks == column // tokens)
    turn = jnp.where(turned, 1.0, 0.0).astype(jnp.bfloat16)
    for head, sum_ref in enumerate(sum_refs):
        span = slice(head * part, (head + 1) * part)
        lanes = [
            jnp.concatenate(
                [sum_ref[b, g * tokens : (g + 1) * tokens, :] for b in range(blocks)], axis=0
            )
            for g in range(TILE)
        ]
        block_rows = jnp.concatenate(lanes, axis=1).astype(jnp.bfloat16)
        token_rows = jnp.dot(turn, block_rows, preferred_element_type=jnp.float32)
        for t in range(tokens):
            base_ref[t, :, span] = token_rows[t * blocks : (t + 1) * blocks].astype(jnp.bfloat16)


def merge_pages(block_of, steps, parts, like):
    count = len(steps)
    tokens, blocks, width = like.shape
    kv_heads = width // (TILE * HEAD_DIM)
    size = TILE * tokens
    vmem = pl.BlockSpec(memory_space=pltpu.VMEM)
    stats = jax.ShapeDtypeStruct((blocks, kv_heads, size), jnp.float32)
    sums = jax.ShapeDtypeStruct((blocks, size, HEAD_DIM), jnp.float32)
    return pl.pallas_call(
        functools.partial(merge_kernel, steps),
        out_shape=[jax.ShapeDtypeStruct(like.shape, jnp.bfloat16), stats, stats]
        + [sums] * kv_heads,
        in_specs=[pl.BlockSpec(memory_space=pltpu.SMEM)] + [vmem] * count,
        out_specs=[vmem] * (3 + kv_heads),
        compiler_params=pltpu.CompilerParams(vmem_limit_bytes=VMEM_BYTES),
        cost_estimate=pl.CostEstimate(flops=0, bytes_accessed=4 << 20, transcendentals=0),
        name="merge_pages",
    )(block_of, *[parts[step] for step in steps])


def settle_kernel(steps, block_ref, base_ref, top_ref, total_ref, *refs):
    count = len(steps)
    parts, sum_refs = refs[:count], refs[count:-3]
    out_ref, done_ref, leaving = refs[-3:]
    tokens, blocks, width = out_ref.shape
    size = TILE * tokens
    part = TILE * HEAD_DIM
    kv_heads = width // part
    asking = [block_ref[step] for step in steps]
    logs = [unpack_logs(ref, kv_heads) for ref in parts]
    shares = []
    for block in asking:
        old = top_ref[block]
        own = [jnp.where(asking[n] == block, logs[n], -1e30) for n in range(count)]
        top = functools.reduce(jnp.maximum, own, old)
        weights = [jnp.exp(old - top) * total_ref[block]] + [jnp.exp(log - top) for log in own]
        total = sum(weights)
        shares += [weight / total for weight in weights]
    columns = as_columns(shares)
    row = lax.broadcasted_iota(jnp.int32, (tokens * blocks, count * tokens), 0)
    column = lax.broadcasted_iota(jnp.int32, (tokens * blocks, count * tokens), 1)
    turned = jnp.zeros(row.shape, jnp.bool_)
    block_row = lax.broadcasted_iota(jnp.int32, (blocks, part), 0)
    fresh = jnp.zeros((blocks, part), jnp.bool_)
    for n, block in enumerate(asking):
        first = jnp.bool_(True)
        for m in range(n):
            first = first & (asking[m] != block)
        wanted = jnp.where(first, block, -1)
        turned = turned | (
            (row // blocks == column - n * tokens) & (row % blocks == wanted)
        )
        fresh = fresh | (block_row == block)
    turn = jnp.where(turned, 1.0, 0.0).astype(jnp.bfloat16)
    copies = []
    for head, sum_ref in enumerate(sum_refs):
        span = slice(head * part, (head + 1) * part)
        merged = []
        for n, block in enumerate(asking):
            rows = [sum_ref[block]]
            rows += [ref[head * size : (head + 1) * size, :].astype(jnp.float32) for ref in parts]
            total = None
            for m, value in enumerate(rows):
                place = (n * (count + 1) + m) * kv_heads + head
                term = columns[:size, place : place + 1] * value
                total = term if total is None else total + term
            merged.append(total)
        lanes = [
            jnp.concatenate([rows[g * tokens : (g + 1) * tokens, :] for rows in merged], axis=0)
            for g in range(TILE)
        ]
        block_rows = jnp.concatenate(lanes, axis=1).astype(jnp.bfloat16)
        token_rows = jnp.dot(turn, block_rows, preferred_element_type=jnp.float32)
        for t in range(tokens):
            new = token_rows[t * blocks : (t + 1) * blocks]
            old = base_ref[t, :, span].astype(jnp.float32)
            done_ref[t, :, span] = jnp.where(fresh, new, old).astype(jnp.bfloat16)
        copy = pltpu.make_async_copy(
            done_ref.at[:, :, span], out_ref.at[:, :, span], leaving.at[head]
        )
        copy.start()
        copies.append(copy)
    for copy in copies:
        copy.wait()


def settle_pages(block_of, merged, steps, parts):
    count = len(steps)
    base, top, total, *sums = merged
    vmem = pl.BlockSpec(memory_space=pltpu.VMEM)
    return pl.pallas_call(
        functools.partial(settle_kernel, steps),
        out_shape=jax.ShapeDtypeStruct(base.shape, jnp.bfloat16),
        in_specs=[pl.BlockSpec(memory_space=pltpu.SMEM)] + [vmem] * (3 + count + len(sums)),
        out_specs=pl.BlockSpec(memory_space=pltpu.HBM),
        scratch_shapes=[
            pltpu.VMEM(base.shape, jnp.bfloat16),
            pltpu.SemaphoreType.DMA((len(sums),)),
        ],
        compiler_params=pltpu.CompilerParams(vmem_limit_bytes=VMEM_BYTES),
        cost_estimate=pl.CostEstimate(flops=0, bytes_accessed=4 << 20, transcendentals=0),
        name="settle_pages",
    )(block_of, base, top, total, *[parts[step] for step in steps], *sums)


class Window:
    def __init__(self, far, depth):
        self.far, self.depth = far, depth
        self.arrived = {False: [], True: []}

    def swap(self, value, step):
        if step == 0:
            return value
        arrived = self.arrived[step >= self.far]
        if len(arrived) >= self.depth:
            value, _ = lax.optimization_barrier((value, arrived[-self.depth]))
        count = lax.axis_size("ctx")
        pairs = [(source, source ^ step) for source in range(count)]
        arrived.append(lax.ppermute(value, "ctx", pairs))
        return arrived[-1]


def stepped_body(queries, kv_cache, page_counts, doc_ids):
    every = tuple(range(lax.axis_size("ctx")))
    early = (8, 9)
    late = tuple(step for step in every if step not in early)
    _, first = pack_queries(queries, page_counts, doc_ids, early, early)
    block_of, rest = pack_queries(queries, page_counts, doc_ids, late, every)
    sent = dict(zip(early + late, first + rest))
    window = Window(len(every) // 2, 3)
    asked, parts = {}, {}

    def ask(*steps):
        for step in steps:
            asked[step] = window.swap(sent[step], step)

    def attend(*steps):
        for step, part in zip(steps, attend_page(kv_cache[0], [asked[s] for s in steps])):
            parts[step] = part

    def answer(*steps):
        for step in steps:
            parts[step] = window.swap(parts[step], step)

    ask(8, 9, 1, 10, 11, 2, 4, 12, 13, 3, 14, 5, 15, 6, 7, 0)
    attend(0, 1, 2, 3)
    attend(8, 9, 10, 11)
    answer(8, 9, 1, 10, 2)
    attend(4, 5, 6, 7)
    answer(11, 4, 3)
    attend(12, 13, 14, 15)
    answer(12, 5, 13, 6, 14, 7, 15)
    last = (7, 15)
    before = tuple(step for step in every if step not in last)
    merged = merge_pages(block_of, before, parts, queries)
    return settle_pages(block_of, merged, last, parts)


def body(queries, kv_cache, page_counts, doc_ids):
    tokens, blocks, width = queries.shape
    groups = width // kv_cache.shape[-1]
    fits = tokens == TILE and blocks == TILE and groups == TILE and lax.axis_size("ctx") == 2 * TILE
    chosen = stepped_body if fits else gathered_body
    return chosen(queries, kv_cache, page_counts, doc_ids)


def solution(mesh):
    placed = (
        P(("group", "ctx"), None, None),
        P(("group", "ctx"), None, None, None),
        P("group"),
        P("group"),
    )
    return jax.shard_map(
        body, mesh=mesh, in_specs=placed, out_specs=P(("group", "ctx"), None, None), check_vma=False
    )
```

```python
import functools
import math

import jax
import jax.numpy as jnp
from jax import lax
from jax.experimental import pallas as pl
from jax.experimental.pallas import tpu as pltpu
from jax.sharding import PartitionSpec as P

HEAD_DIM = 128
TILE = 8
STAT_ROWS = 16
SLOTS = 3
VMEM_BYTES = 32 * 1024 * 1024


def doc_of(pages, doc_ends):
    return jnp.sum((pages[..., None] >= doc_ends).astype(jnp.int32), axis=-1)


def page_partial(rows, page_kv):
    tokens = rows.shape[0]
    kv_heads = page_kv.shape[-1] // HEAD_DIM
    groups = rows.shape[-1] // (kv_heads * HEAD_DIM)
    grouped = rows.reshape(tokens, kv_heads, groups, HEAD_DIM)
    keys = page_kv[0].reshape(-1, kv_heads, HEAD_DIM)
    values = page_kv[1].reshape(-1, kv_heads, HEAD_DIM)
    scores = jnp.einsum(
        "qhgd,khd->qhgk", grouped, keys, preferred_element_type=jnp.float32
    ) * HEAD_DIM ** (-0.5)
    row_max = jnp.max(scores, axis=-1)
    expo = jnp.exp(scores - row_max[..., None])
    row_sum = jnp.sum(expo, axis=-1)
    weights = expo.astype(jnp.bfloat16)
    mixed = jnp.einsum("qhgk,khd->qhgd", weights, values, preferred_element_type=jnp.float32)
    return (row_max.reshape(tokens, -1), row_sum.reshape(tokens, -1), mixed.reshape(tokens, -1))


def page_blocks(pages, page_counts, doc_ids):
    block_order = jnp.arange(doc_ids.shape[0], dtype=jnp.int32)
    page_docs = doc_of(pages, jnp.cumsum(page_counts))
    return jnp.sum(jnp.where(doc_ids == page_docs[:, None], block_order, 0), axis=-1)


def gathered_body(queries, kv_cache, page_counts, doc_ids):
    peers = lax.axis_size("ctx")
    local_rows, blocks, width = queries.shape
    heads = width // HEAD_DIM
    block_of = page_blocks(jnp.arange(peers, dtype=jnp.int32), page_counts, doc_ids)
    outgoing = jnp.take(queries, block_of, axis=1)
    arrived = lax.all_to_all(outgoing, "ctx", split_axis=1, concat_axis=0, tiled=True)
    row_max, row_sum, mixed = page_partial(arrived.reshape(-1, width), kv_cache[0])
    send = [part.reshape(peers, local_rows, -1) for part in (mixed, row_max, row_sum)]
    got_out, got_max, got_sum = [
        lax.all_to_all(part, "ctx", split_axis=0, concat_axis=0, tiled=True) for part in send
    ]
    matches = (block_of == jnp.arange(blocks, dtype=jnp.int32)[:, None])[..., None, None]
    masked = jnp.where(matches, got_max, -1e30)
    row_top = jnp.max(masked, axis=1, keepdims=True)
    weight = jnp.where(matches, jnp.exp(masked - row_top), 0.0)
    denominator = jnp.sum(weight * got_sum, axis=1)
    numerator = jnp.einsum(
        "cnrh,nrhd->crhd",
        weight,
        got_out.reshape(peers, local_rows, heads, HEAD_DIM),
        precision=lax.Precision.HIGHEST,
    )
    mixed_out = (numerator / denominator[..., None]).reshape(blocks, local_rows, width)
    return jnp.moveaxis(mixed_out, 0, 1).astype(jnp.bfloat16)


def pack_kernel(steps, listed, counts_hbm, ids_hbm, query_ref, block_ref, *refs):
    count = len(steps)
    sent_refs, (rows_ref, counts_ref, ids_ref, arrival, read) = refs[:count], refs[count:]
    small = [
        pltpu.make_async_copy(counts_hbm, counts_ref, read.at[0]),
        pltpu.make_async_copy(ids_hbm, ids_ref, read.at[1]),
    ]
    for copy in small:
        copy.start()
    tokens, blocks, width = query_ref.shape
    part = TILE * HEAD_DIM
    heads = range(width // part)
    spans = [slice(head * part, (head + 1) * part) for head in heads]
    copies = [
        pltpu.make_async_copy(query_ref.at[:, :, span], rows_ref.at[:, :, span], arrival.at[head])
        for head, span in zip(heads, spans)
    ]
    for copy in copies:
        copy.start()
    for copy in small:
        copy.wait()
    own = lax.axis_index("ctx")
    ends, end = [], 0
    for doc in range(blocks):
        end = end + counts_ref[doc]
        ends.append(end)
    ids = [ids_ref[block] for block in range(blocks)]
    asking = {}
    for n, step in enumerate(listed):
        page = own ^ step
        doc = sum((page >= end).astype(jnp.int32) for end in ends)
        block = sum(jnp.where(ids[c] == doc, c, 0) for c in range(1, blocks))
        block_ref[n] = block
        asking[step] = block
    row = lax.broadcasted_iota(jnp.int32, (tokens, tokens * blocks), 0)
    column = lax.broadcasted_iota(jnp.int32, (tokens, tokens * blocks), 1)
    pick = jnp.concatenate(
        [jnp.where(column == row * blocks + asking[step], 1.0, 0.0) for step in steps], axis=0
    ).astype(jnp.bfloat16)
    size = TILE * tokens
    for head in heads:
        copies[head].wait()
        rows = jnp.concatenate(
            [rows_ref[t, :, spans[head]].astype(jnp.float32) for t in range(tokens)], axis=0
        ).astype(jnp.bfloat16)
        picked = jnp.dot(pick, rows, preferred_element_type=jnp.float32)
        for n in range(count):
            own_rows = picked[n * tokens : (n + 1) * tokens]
            own_rows = jnp.concatenate(
                [own_rows[:, g * HEAD_DIM : (g + 1) * HEAD_DIM] for g in range(TILE)], axis=0
            )
            sent_refs[n][head * size : (head + 1) * size, :] = own_rows.astype(jnp.bfloat16)


def pack_queries(queries, page_counts, doc_ids, steps, listed):
    count = len(steps)
    tokens, _, width = queries.shape
    rows = tokens * width // HEAD_DIM
    vmem, smem = pl.BlockSpec(memory_space=pltpu.VMEM), pl.BlockSpec(memory_space=pltpu.SMEM)
    hbm = pl.BlockSpec(memory_space=pltpu.HBM)
    block_of, *sent = pl.pallas_call(
        functools.partial(pack_kernel, steps, listed),
        out_shape=[jax.ShapeDtypeStruct((len(listed),), jnp.int32)]
        + [jax.ShapeDtypeStruct((rows, HEAD_DIM), jnp.bfloat16)] * count,
        in_specs=[hbm, hbm, hbm],
        out_specs=[smem] + [vmem] * count,
        scratch_shapes=[
            pltpu.VMEM(queries.shape, jnp.bfloat16),
            pltpu.SMEM(page_counts.shape, jnp.int32),
            pltpu.SMEM(doc_ids.shape, jnp.int32),
            pltpu.SemaphoreType.DMA((width // (TILE * HEAD_DIM),)),
            pltpu.SemaphoreType.DMA((2,)),
        ],
        cost_estimate=pl.CostEstimate(flops=0, bytes_accessed=4 << 20, transcendentals=0),
        name="pack_queries",
    )(page_counts, doc_ids, queries)
    return block_of, sent


def attend_kernel(count, kv_ref, *refs):
    asked, answers, log_ref = refs[:count], refs[count : 2 * count], refs[2 * count]
    kv_heads = kv_ref.shape[2] // HEAD_DIM
    size = asked[0].shape[0] // kv_heads
    scale = HEAD_DIM ** (-0.5)

    for head in range(kv_heads):
        lanes = slice(head * HEAD_DIM, (head + 1) * HEAD_DIM)
        rows = slice(head * size, (head + 1) * size)
        query = jnp.concatenate([ref[rows, :] for ref in asked], axis=0)
        scores = lax.dot_general(
            kv_ref[0, :, lanes], query, (((1,), (1,)), ((), ())), preferred_element_type=jnp.float32
        )
        top = jnp.max(scores, axis=0, keepdims=True)
        expo = jnp.exp2((scores - top) * (scale / math.log(2.0)))
        total = jnp.sum(expo, axis=0, keepdims=True)
        mixed = lax.dot_general(
            expo.astype(jnp.bfloat16),
            kv_ref[1, :, lanes],
            (((0,), (0,)), ((), ())),
            preferred_element_type=jnp.float32,
        )
        mixed = mixed * jnp.transpose(jnp.broadcast_to(1.0 / total, (HEAD_DIM, total.shape[1])))
        for n in range(count):
            answers[n][rows, :] = mixed[n * size : (n + 1) * size].astype(jnp.bfloat16)
        log_ref[head : head + 1, :] = top * scale + jnp.log(total)
    logs = log_ref[...]
    high = logs.astype(jnp.bfloat16).astype(jnp.float32)
    middle = (logs - high).astype(jnp.bfloat16).astype(jnp.float32)
    low = logs - high - middle
    for n in range(count):
        span = slice(n * size, (n + 1) * size)
        upper = jnp.concatenate([high[:, span], middle[:, span]], axis=1)
        lower = jnp.concatenate([low[:, span], jnp.zeros_like(low[:, span])], axis=1)
        answers[n][kv_heads * size :, :] = jnp.concatenate([upper, lower], axis=0).astype(
            jnp.bfloat16
        )


def attend_page(page_kv, asked):
    count = len(asked)
    rows = asked[0].shape[0]
    kv_heads = page_kv.shape[2] // HEAD_DIM
    flops = 4 * count * rows * page_kv.shape[1] * HEAD_DIM
    return pl.pallas_call(
        functools.partial(attend_kernel, count),
        out_shape=[jax.ShapeDtypeStruct((rows + STAT_ROWS, HEAD_DIM), jnp.bfloat16)] * count,
        in_specs=[pl.BlockSpec(memory_space=pltpu.VMEM)] * (1 + count),
        out_specs=[pl.BlockSpec(memory_space=pltpu.VMEM)] * count,
        scratch_shapes=[pltpu.VMEM((kv_heads, count * rows // kv_heads), jnp.float32)],
        compiler_params=pltpu.CompilerParams(vmem_limit_bytes=VMEM_BYTES),
        cost_estimate=pl.CostEstimate(
            flops=flops, bytes_accessed=3 << 20, transcendentals=flops // 512
        ),
        name="attend_page",
    )(page_kv, *asked)


def unpack_logs(part_ref, kv_heads):
    stat = part_ref[part_ref.shape[0] - STAT_ROWS :, :].astype(jnp.float32)
    size = stat.shape[1] // 2
    return stat[:kv_heads, :size] + stat[:kv_heads, size:] + stat[kv_heads:, :size]


def as_columns(shares):
    rows = jnp.concatenate(shares, axis=0)
    rows = jnp.concatenate([rows, jnp.zeros_like(rows)], axis=1)
    missing = HEAD_DIM - rows.shape[0] % HEAD_DIM
    if missing < HEAD_DIM:
        rows = jnp.concatenate([rows, jnp.zeros((missing, rows.shape[1]), jnp.float32)], axis=0)
    return jnp.transpose(rows)


def merge_kernel(steps, block_ref, *refs):
    count = len(steps)
    parts, (base_ref, top_ref, total_ref) = refs[:count], refs[count : count + 3]
    sum_refs = refs[count + 3 :]
    tokens, blocks, width = base_ref.shape
    size = TILE * tokens
    part = TILE * HEAD_DIM
    kv_heads = width // part
    top_ref[...] = jnp.full(top_ref.shape, -1e30, jnp.float32)
    total_ref[...] = jnp.zeros(total_ref.shape, jnp.float32)
    for sum_ref in sum_refs:
        sum_ref[...] = jnp.zeros(sum_ref.shape, jnp.float32)
    asking = [block_ref[step] for step in steps]
    logs = [unpack_logs(parts[n], kv_heads) for n in range(count)]
    for n in range(count):
        top_ref[asking[n]] = jnp.maximum(top_ref[asking[n]], logs[n])
    shares = [jnp.exp(logs[n] - top_ref[asking[n]]) for n in range(count)]
    for n in range(count):
        total_ref[asking[n]] += shares[n]
    columns = as_columns([shares[n] / total_ref[asking[n]] for n in range(count)])
    for n in range(count):
        for head, sum_ref in enumerate(sum_refs):
            place = n * kv_heads + head
            share = columns[:size, place : place + 1]
            part_rows = parts[n][head * size : (head + 1) * size, :]
            sum_ref[asking[n]] += share * part_rows.astype(jnp.float32)
    row = lax.broadcasted_iota(jnp.int32, (tokens * blocks, tokens * blocks), 0)
    column = lax.broadcasted_iota(jnp.int32, (tokens * blocks, tokens * blocks), 1)
    turned = (row // blocks == column % tokens) & (row % blocks == column // tokens)
    turn = jnp.where(turned, 1.0, 0.0).astype(jnp.bfloat16)
    for head, sum_ref in enumerate(sum_refs):
        span = slice(head * part, (head + 1) * part)
        lanes = [
            jnp.concatenate(
                [sum_ref[b, g * tokens : (g + 1) * tokens, :] for b in range(blocks)], axis=0
            )
            for g in range(TILE)
        ]
        block_rows = jnp.concatenate(lanes, axis=1).astype(jnp.bfloat16)
        token_rows = jnp.dot(turn, block_rows, preferred_element_type=jnp.float32)
        for t in range(tokens):
            base_ref[t, :, span] = token_rows[t * blocks : (t + 1) * blocks].astype(jnp.bfloat16)


def merge_pages(block_of, steps, parts, like):
    count = len(steps)
    tokens, blocks, width = like.shape
    kv_heads = width // (TILE * HEAD_DIM)
    size = TILE * tokens
    vmem = pl.BlockSpec(memory_space=pltpu.VMEM)
    stats = jax.ShapeDtypeStruct((blocks, kv_heads, size), jnp.float32)
    sums = jax.ShapeDtypeStruct((blocks, size, HEAD_DIM), jnp.float32)
    return pl.pallas_call(
        functools.partial(merge_kernel, steps),
        out_shape=[jax.ShapeDtypeStruct(like.shape, jnp.bfloat16), stats, stats]
        + [sums] * kv_heads,
        in_specs=[pl.BlockSpec(memory_space=pltpu.SMEM)] + [vmem] * count,
        out_specs=[vmem] * (3 + kv_heads),
        compiler_params=pltpu.CompilerParams(vmem_limit_bytes=VMEM_BYTES),
        cost_estimate=pl.CostEstimate(flops=0, bytes_accessed=4 << 20, transcendentals=0),
        name="merge_pages",
    )(block_of, *[parts[step] for step in steps])


def settle_kernel(steps, block_ref, base_ref, top_ref, total_ref, *refs):
    count = len(steps)
    parts, sum_refs = refs[:count], refs[count:-3]
    out_ref, done_ref, leaving = refs[-3:]
    tokens, blocks, width = out_ref.shape
    size = TILE * tokens
    part = TILE * HEAD_DIM
    kv_heads = width // part
    asking = [block_ref[step] for step in steps]
    logs = [unpack_logs(ref, kv_heads) for ref in parts]
    shares = []
    for block in asking:
        old = top_ref[block]
        own = [jnp.where(asking[n] == block, logs[n], -1e30) for n in range(count)]
        top = functools.reduce(jnp.maximum, own, old)
        weights = [jnp.exp(old - top) * total_ref[block]] + [jnp.exp(log - top) for log in own]
        total = sum(weights)
        shares += [weight / total for weight in weights]
    columns = as_columns(shares)
    row = lax.broadcasted_iota(jnp.int32, (tokens * blocks, count * tokens), 0)
    column = lax.broadcasted_iota(jnp.int32, (tokens * blocks, count * tokens), 1)
    turned = jnp.zeros(row.shape, jnp.bool_)
    block_row = lax.broadcasted_iota(jnp.int32, (blocks, part), 0)
    fresh = jnp.zeros((blocks, part), jnp.bool_)
    for n, block in enumerate(asking):
        first = jnp.bool_(True)
        for m in range(n):
            first = first & (asking[m] != block)
        wanted = jnp.where(first, block, -1)
        turned = turned | (
            (row // blocks == column - n * tokens) & (row % blocks == wanted)
        )
        fresh = fresh | (block_row == block)
    turn = jnp.where(turned, 1.0, 0.0).astype(jnp.bfloat16)
    copies = []
    for head, sum_ref in enumerate(sum_refs):
        span = slice(head * part, (head + 1) * part)
        merged = []
        for n, block in enumerate(asking):
            rows = [sum_ref[block]]
            rows += [ref[head * size : (head + 1) * size, :].astype(jnp.float32) for ref in parts]
            total = None
            for m, value in enumerate(rows):
                place = (n * (count + 1) + m) * kv_heads + head
                term = columns[:size, place : place + 1] * value
                total = term if total is None else total + term
            merged.append(total)
        lanes = [
            jnp.concatenate([rows[g * tokens : (g + 1) * tokens, :] for rows in merged], axis=0)
            for g in range(TILE)
        ]
        block_rows = jnp.concatenate(lanes, axis=1).astype(jnp.bfloat16)
        token_rows = jnp.dot(turn, block_rows, preferred_element_type=jnp.float32)
        for t in range(tokens):
            new = token_rows[t * blocks : (t + 1) * blocks]
            old = base_ref[t, :, span].astype(jnp.float32)
            done_ref[t, :, span] = jnp.where(fresh, new, old).astype(jnp.bfloat16)
        copy = pltpu.make_async_copy(
            done_ref.at[:, :, span], out_ref.at[:, :, span], leaving.at[head]
        )
        copy.start()
        copies.append(copy)
    for copy in copies:
        copy.wait()


def settle_pages(block_of, merged, steps, parts):
    count = len(steps)
    base, top, total, *sums = merged
    vmem = pl.BlockSpec(memory_space=pltpu.VMEM)
    return pl.pallas_call(
        functools.partial(settle_kernel, steps),
        out_shape=jax.ShapeDtypeStruct(base.shape, jnp.bfloat16),
        in_specs=[pl.BlockSpec(memory_space=pltpu.SMEM)] + [vmem] * (3 + count + len(sums)),
        out_specs=pl.BlockSpec(memory_space=pltpu.HBM),
        scratch_shapes=[
            pltpu.VMEM(base.shape, jnp.bfloat16),
            pltpu.SemaphoreType.DMA((len(sums),)),
        ],
        compiler_params=pltpu.CompilerParams(vmem_limit_bytes=VMEM_BYTES),
        cost_estimate=pl.CostEstimate(flops=0, bytes_accessed=4 << 20, transcendentals=0),
        name="settle_pages",
    )(block_of, base, top, total, *[parts[step] for step in steps], *sums)


class Window:
    def __init__(self, far, depth):
        self.far, self.depth = far, depth
        self.arrived = {False: [], True: []}

    def swap(self, value, step):
        if step == 0:
            return value
        arrived = self.arrived[step >= self.far]
        if len(arrived) >= self.depth:
            value, _ = lax.optimization_barrier((value, arrived[-self.depth]))
        count = lax.axis_size("ctx")
        pairs = [(source, source ^ step) for source in range(count)]
        arrived.append(lax.ppermute(value, "ctx", pairs))
        return arrived[-1]


def stepped_body(queries, kv_cache, page_counts, doc_ids):
    every = tuple(range(lax.axis_size("ctx")))
    early = (8, 9)
    late = tuple(step for step in every if step not in early)
    _, first = pack_queries(queries, page_counts, doc_ids, early, early)
    block_of, rest = pack_queries(queries, page_counts, doc_ids, late, every)
    sent = dict(zip(early + late, first + rest))
    window = Window(len(every) // 2, 3)
    asked, parts = {}, {}

    def ask(*steps):
        for step in steps:
            asked[step] = window.swap(sent[step], step)

    def attend(*steps):
        for step, part in zip(steps, attend_page(kv_cache[0], [asked[s] for s in steps])):
            parts[step] = part

    def answer(*steps):
        for step in steps:
            parts[step] = window.swap(parts[step], step)

    ask(8, 9, 1, 10, 11, 2, 4, 12, 13, 3, 14, 5, 15, 6, 7, 0)
    attend(0, 1, 2, 3)
    attend(8, 9, 10, 11)
    answer(8, 9, 1, 10, 2)
    attend(4, 5, 6, 7)
    answer(11, 4, 3)
    attend(12, 13, 14, 15)
    answer(12, 5, 13, 6, 14, 7, 15)
    last = (7, 15)
    before = tuple(step for step in every if step not in last)
    merged = merge_pages(block_of, before, parts, queries)
    return settle_pages(block_of, merged, last, parts)


def table_kernel(levels, counts_hbm, ids_hbm, table_ref, most_ref, counts_ref, ids_ref, read):
    small = [
        pltpu.make_async_copy(counts_hbm, counts_ref, read.at[0]),
        pltpu.make_async_copy(ids_hbm, ids_ref, read.at[1]),
    ]
    for copy in small:
        copy.start()
    for copy in small:
        copy.wait()
    docs = counts_ref.shape[0]
    ends, end = [], 0
    for doc in range(docs):
        end = end + counts_ref[doc]
        ends.append(end)
    ids = [ids_ref[block] for block in range(docs)]
    most = 0
    for level in range(levels):
        found = [
            sum((level * 4 + n >= end).astype(jnp.int32) for end in ends) for n in range(4)
        ]
        most = jnp.maximum(most, found[3] - found[0] + 1)
        for n in range(4):
            doc = jnp.minimum(found[0] + n, docs - 1)
            block = sum(jnp.where(ids[c] == doc, c, 0) for c in range(1, docs))
            table_ref[level * 4 + n] = block
            table_ref[levels * 4 + level * 4 + n] = found[n] - found[0]
    most_ref[0] = most


def level_table(page_counts, doc_ids, levels):
    hbm = pl.BlockSpec(memory_space=pltpu.HBM)
    return pl.pallas_call(
        functools.partial(table_kernel, levels),
        out_shape=[
            jax.ShapeDtypeStruct((levels * 8,), jnp.int32),
            jax.ShapeDtypeStruct((1,), jnp.int32),
        ],
        in_specs=[hbm, hbm],
        out_specs=[pl.BlockSpec(memory_space=pltpu.SMEM)] * 2,
        scratch_shapes=[
            pltpu.SMEM(page_counts.shape, jnp.int32),
            pltpu.SMEM(doc_ids.shape, jnp.int32),
            pltpu.SemaphoreType.DMA((2,)),
        ],
        name="level_table",
    )(page_counts, doc_ids)


def own_place():
    own = lax.axis_index("ctx")
    return own >> 2, own & 3


def split_kernel(kv_ref, *refs):
    _, role = own_place()
    pieces, done = refs[:4], refs[4]
    width = pieces[0].shape[2]
    copies = []
    for step, piece_ref in enumerate(pieces):
        lanes = pl.ds(pl.multiple_of((role ^ step) * width, width), width)
        copies.append(pltpu.make_async_copy(kv_ref.at[:, :, lanes], piece_ref, done.at[step]))
    for copy in copies:
        copy.start()
    for copy in copies:
        copy.wait()


def split_heads(page_kv):
    shape = (2, page_kv.shape[1], page_kv.shape[2] // 4)
    return pl.pallas_call(
        split_kernel,
        out_shape=[jax.ShapeDtypeStruct(shape, jnp.bfloat16)] * 4,
        in_specs=[pl.BlockSpec(memory_space=pltpu.HBM)],
        out_specs=[pl.BlockSpec(memory_space=pltpu.VMEM)] * 4,
        scratch_shapes=[pltpu.SemaphoreType.DMA((4,))],
        cost_estimate=pl.CostEstimate(flops=0, bytes_accessed=4 << 20, transcendentals=0),
        name="split_heads",
    )(page_kv)


def slot_kernel(steps, table_ref, query_ref, *refs):
    count = len(steps)
    reached = [(n, side, step | side) for n, step in enumerate(steps) for side in range(2)]
    sent_refs, rows_ref, arrival = refs[:count], refs[count], refs[count + 1]
    level, role = own_place()
    tokens, blocks, _ = query_ref.shape
    part = TILE * HEAD_DIM
    size = TILE * tokens
    shifts = sorted({step & 3 for _, _, step in reached})
    copies = {}
    for shift in shifts:
        lanes = pl.ds(pl.multiple_of((role ^ shift) * 2 * part, 2 * part), 2 * part)
        copies[shift] = pltpu.make_async_copy(
            query_ref.at[:, :, lanes], rows_ref.at[shift], arrival.at[shift]
        )
        copies[shift].start()
    row = lax.broadcasted_iota(jnp.int32, (tokens, tokens * blocks), 0)
    column = lax.broadcasted_iota(jnp.int32, (tokens, tokens * blocks), 1)
    picks = {}
    for far in sorted({step >> 2 for _, _, step in reached}):
        picks[far] = [
            jnp.where(column == row * blocks + table_ref[(level ^ far) * 4 + slot], 1.0, 0.0)
            for slot in range(SLOTS)
        ]
    for shift in shifts:
        own = [(n, side, step >> 2) for n, side, step in reached if step & 3 == shift]
        pick = jnp.concatenate([p for _, _, far in own for p in picks[far]], axis=0)
        pick = pick.astype(jnp.bfloat16)
        copies[shift].wait()
        for head in range(2):
            span = slice(head * part, (head + 1) * part)
            rows = jnp.concatenate(
                [rows_ref[shift, t, :, span].astype(jnp.float32) for t in range(tokens)], axis=0
            ).astype(jnp.bfloat16)
            picked = jnp.dot(pick, rows, preferred_element_type=jnp.float32)
            for m, (n, side, _) in enumerate(own):
                for slot in range(SLOTS):
                    first = (m * SLOTS + slot) * tokens
                    value = picked[first : first + tokens]
                    value = jnp.concatenate(
                        [value[:, g * HEAD_DIM : (g + 1) * HEAD_DIM] for g in range(TILE)], axis=0
                    )
                    first = ((side * SLOTS + slot) * 2 + head) * size
                    sent_refs[n][first : first + size, :] = value.astype(jnp.bfloat16)


def slot_queries(table, queries, steps):
    tokens, blocks, width = queries.shape
    rows = 2 * SLOTS * 2 * TILE * tokens
    return pl.pallas_call(
        functools.partial(slot_kernel, steps),
        out_shape=[jax.ShapeDtypeStruct((rows, HEAD_DIM), jnp.bfloat16)] * len(steps),
        in_specs=[
            pl.BlockSpec(memory_space=pltpu.SMEM),
            pl.BlockSpec(memory_space=pltpu.HBM),
        ],
        out_specs=[pl.BlockSpec(memory_space=pltpu.VMEM)] * len(steps),
        scratch_shapes=[
            pltpu.VMEM((4, tokens, blocks, width // 4), jnp.bfloat16),
            pltpu.SemaphoreType.DMA((4,)),
        ],
        cost_estimate=pl.CostEstimate(flops=0, bytes_accessed=4 << 20, transcendentals=0),
        name="slot_queries",
    )(table, queries)


def share_kernel(count, levels, table_ref, *refs):
    pieces, asked = refs[:4], refs[4 : 4 + 2 * count]
    answers = refs[4 + 2 * count : 4 + 3 * count]
    score_ref, top_ref, total_ref, sum_ref = refs[4 + 3 * count :]
    level, role = own_place()
    scale = HEAD_DIM ** (-0.5)
    size = asked[1].shape[0] // (2 * SLOTS)
    section = 2 * SLOTS * size + STAT_ROWS
    places = [table_ref[levels * 4 + level * 4 + (role ^ step)] for step in range(4)]
    units = [(step, head) for step in range(4) for head in range(2)]
    top_ref[...] = jnp.full(top_ref.shape, -1e30, jnp.float32)
    total_ref[...] = jnp.zeros(total_ref.shape, jnp.float32)
    sum_ref[...] = jnp.zeros(sum_ref.shape, jnp.float32)
    for unit, (step, head) in enumerate(units):
        place = places[step] * 2 + head
        rows = pl.ds(pl.multiple_of(place * size, size), size)
        query = jnp.concatenate([ref[rows, :] for ref in asked], axis=0)
        keys = pieces[step][0, :, head * HEAD_DIM : (head + 1) * HEAD_DIM]
        scores = lax.dot_general(
            keys, query, (((1,), (1,)), ((), ())), preferred_element_type=jnp.float32
        )
        score_ref[unit] = scores
        line = pl.ds(place, 1)
        top_ref[line, :] = jnp.maximum(top_ref[line, :], jnp.max(scores, axis=0, keepdims=True))
    for unit, (step, head) in enumerate(units):
        place = places[step] * 2 + head
        line = pl.ds(place, 1)
        expo = jnp.exp2((score_ref[unit] - top_ref[line, :]) * (scale / math.log(2.0)))
        total_ref[line, :] += jnp.sum(expo, axis=0, keepdims=True)
        sum_ref[place] += lax.dot_general(
            expo.astype(jnp.bfloat16),
            pieces[step][1, :, head * HEAD_DIM : (head + 1) * HEAD_DIM],
            (((0,), (0,)), ((), ())),
            preferred_element_type=jnp.float32,
        )
    totals = total_ref[...]
    inverse = jnp.where(totals > 0.0, 1.0 / jnp.maximum(totals, 1e-30), 0.0)
    logs = top_ref[...] * scale + jnp.log(jnp.maximum(totals, 1e-30))
    high = logs.astype(jnp.bfloat16).astype(jnp.float32)
    middle = (logs - high).astype(jnp.bfloat16).astype(jnp.float32)
    low = logs - high - middle
    for place in range(2 * SLOTS):
        column = jnp.broadcast_to(inverse[place : place + 1], (HEAD_DIM, inverse.shape[1]))
        mixed = sum_ref[place] * jnp.transpose(column)
        for n in range(2 * count):
            value = mixed[n * size : (n + 1) * size].astype(jnp.bfloat16)
            first = (n % 2) * section + place * size
            answers[n // 2][first : first + size, :] = value
    for n in range(2 * count):
        span = slice(n * size, (n + 1) * size)
        upper = jnp.concatenate([high[:, span], middle[:, span]], axis=1)
        lower = jnp.concatenate([low[:, span], jnp.zeros_like(low[:, span])], axis=1)
        last = (n % 2 + 1) * section
        answers[n // 2][last - STAT_ROWS : last, :] = jnp.concatenate(
            [upper, lower], axis=0
        ).astype(jnp.bfloat16)


def share_pages(table, pieces, asked, levels):
    count = len(asked) // 2
    rows = asked[1].shape[0]
    columns = 2 * count * rows // (2 * SLOTS)
    page_tokens = pieces[0].shape[1]
    smem, vmem = pl.BlockSpec(memory_space=pltpu.SMEM), pl.BlockSpec(memory_space=pltpu.VMEM)
    flops = 4 * 8 * columns * page_tokens * HEAD_DIM
    return pl.pallas_call(
        functools.partial(share_kernel, count, levels),
        out_shape=[jax.ShapeDtypeStruct((2 * (rows + STAT_ROWS), HEAD_DIM), jnp.bfloat16)] * count,
        in_specs=[smem] + [vmem] * (4 + 2 * count),
        out_specs=[vmem] * count,
        scratch_shapes=[
            pltpu.VMEM((8, page_tokens, columns), jnp.float32),
            pltpu.VMEM((8, columns), jnp.float32),
            pltpu.VMEM((8, columns), jnp.float32),
            pltpu.VMEM((2 * SLOTS, columns, HEAD_DIM), jnp.float32),
        ],
        compiler_params=pltpu.CompilerParams(vmem_limit_bytes=VMEM_BYTES),
        cost_estimate=pl.CostEstimate(
            flops=flops, bytes_accessed=3 << 20, transcendentals=flops // 512
        ),
        name="share_pages",
    )(table, *pieces, *asked)


def join_kernel(levels, table_ref, *refs):
    count = levels * 4
    parts, (out_ref, top_ref, total_ref, done_ref, leaving) = refs[:count], refs[count : count + 5]
    sum_refs = refs[count + 5 :]
    level, role = own_place()
    tokens, blocks, _ = out_ref.shape
    size = TILE * tokens
    part = TILE * HEAD_DIM
    top_ref[...] = jnp.full(top_ref.shape, -1e30, jnp.float32)
    total_ref[...] = jnp.zeros(total_ref.shape, jnp.float32)
    for sum_ref in sum_refs:
        sum_ref[...] = jnp.zeros(sum_ref.shape, jnp.float32)
    pairs = [(far, slot) for far in range(levels) for slot in range(SLOTS)]
    asking = [table_ref[(level ^ far) * 4 + slot] for far, slot in pairs]
    section = 2 * SLOTS * size + STAT_ROWS
    stats = [unpack_logs(ref.at[:section, :], 8) for ref in parts]
    logs = [
        jnp.concatenate(
            [stats[far * 4 + shift][2 * slot : 2 * slot + 2] for shift in range(4)], axis=0
        )
        for far, slot in pairs
    ]
    for block, log in zip(asking, logs):
        top_ref[block] = jnp.maximum(top_ref[block], log)
    shares = [jnp.exp(log - top_ref[block]) for block, log in zip(asking, logs)]
    for block, share in zip(asking, shares):
        total_ref[block] += share
    columns = as_columns([share / total_ref[block] for block, share in zip(asking, shares)])
    for n, (far, slot) in enumerate(pairs):
        for head, sum_ref in enumerate(sum_refs):
            share = columns[:size, n * 8 + head : n * 8 + head + 1]
            first = (slot * 2 + head % 2) * size
            value = parts[far * 4 + head // 2][first : first + size, :].astype(jnp.float32)
            sum_ref[asking[n]] += share * value
    row = lax.broadcasted_iota(jnp.int32, (tokens * blocks, tokens * blocks), 0)
    column = lax.broadcasted_iota(jnp.int32, (tokens * blocks, tokens * blocks), 1)
    turned = (row // blocks == column % tokens) & (row % blocks == column // tokens)
    turn = jnp.where(turned, 1.0, 0.0).astype(jnp.bfloat16)
    copies = []
    for head, sum_ref in enumerate(sum_refs):
        lanes = [
            jnp.concatenate(
                [sum_ref[b, g * tokens : (g + 1) * tokens, :] for b in range(blocks)], axis=0
            )
            for g in range(TILE)
        ]
        block_rows = jnp.concatenate(lanes, axis=1).astype(jnp.bfloat16)
        token_rows = jnp.dot(turn, block_rows, preferred_element_type=jnp.float32)
        for t in range(tokens):
            done_ref[head, t] = token_rows[t * blocks : (t + 1) * blocks].astype(jnp.bfloat16)
        place = (role ^ (head // 2)) * 2 + head % 2
        span = pl.ds(pl.multiple_of(place * part, part), part)
        copy = pltpu.make_async_copy(done_ref.at[head], out_ref.at[:, :, span], leaving.at[head])
        copy.start()
        copies.append(copy)
    for copy in copies:
        copy.wait()


def join_levels(table, parts, like, levels):
    smem, vmem = pl.BlockSpec(memory_space=pltpu.SMEM), pl.BlockSpec(memory_space=pltpu.VMEM)
    tokens, blocks, _ = like.shape
    size = TILE * tokens
    return pl.pallas_call(
        functools.partial(join_kernel, levels),
        out_shape=jax.ShapeDtypeStruct(like.shape, jnp.bfloat16),
        in_specs=[smem] + [vmem] * len(parts),
        out_specs=pl.BlockSpec(memory_space=pltpu.HBM),
        scratch_shapes=[
            pltpu.VMEM((blocks, 8, size), jnp.float32),
            pltpu.VMEM((blocks, 8, size), jnp.float32),
            pltpu.VMEM((8, tokens, blocks, TILE * HEAD_DIM), jnp.bfloat16),
            pltpu.SemaphoreType.DMA((8,)),
        ]
        + [pltpu.VMEM((blocks, size, HEAD_DIM), jnp.float32)] * 8,
        compiler_params=pltpu.CompilerParams(vmem_limit_bytes=VMEM_BYTES),
        cost_estimate=pl.CostEstimate(flops=0, bytes_accessed=4 << 20, transcendentals=0),
        name="join_levels",
    )(table, *parts)


def level_body(queries, kv_cache, table):
    levels = lax.axis_size("ctx") // 4
    every = tuple(range(0, levels * 4, 2))
    early = (8,)
    late = tuple(step for step in every if step not in early)
    sent = dict(zip(early, slot_queries(table, queries, early)))
    page_kv, sent[8] = lax.optimization_barrier((kv_cache[0], sent[8]))
    pieces = dict(enumerate(split_heads(page_kv)))
    sent.update(zip(late, slot_queries(table, queries, late)))
    window = Window(len(every), 3)
    held, asked, parts = {}, {}, {}

    def spread(value, step):
        value = window.swap(value, step)
        return value, swapped(value[value.shape[0] // 2 :], 1)

    def fetch(*steps):
        for step in steps:
            piece = pieces[step]
            held[step] = swapped(piece, step) if step == 1 else window.swap(piece, step)

    def ask(*steps):
        for step in steps:
            asked[step] = spread(sent[step], step)

    def attend(*steps):
        own = [held[step] for step in range(4)]
        rows = [ref for step in steps for ref in asked[step]]
        parts.update(zip(steps, share_pages(table, own, rows, levels)))

    def answer(*steps):
        for step in steps:
            parts[step] = spread(parts[step], step)

    fetch(0)
    ask(0, 8)
    fetch(2, 3, 1)
    ask(12, 4, 14, 6, 10, 2)
    attend(8, 12)
    answer(8, 12)
    attend(0, 2)
    answer(2)
    attend(4, 6)
    answer(4)
    attend(10, 14)
    answer(10, 14, 6, 0)
    received = [ref for step in every for ref in parts[step]]
    return join_levels(table, received, queries, levels)


def swapped(value, step):
    count = lax.axis_size("ctx")
    return lax.ppermute(value, "ctx", [(source, source ^ step) for source in range(count)])


def chosen_body(queries, kv_cache, page_counts, doc_ids):
    levels = lax.axis_size("ctx") // 4
    table, most = level_table(page_counts, doc_ids, levels)
    return lax.cond(
        most.reshape(()) <= SLOTS,
        lambda q, kv, table, counts, ids: level_body(q, kv, table),
        lambda q, kv, table, counts, ids: stepped_body(q, kv, counts, ids),
        queries,
        kv_cache,
        table,
        page_counts,
        doc_ids,
    )


def body(queries, kv_cache, page_counts, doc_ids):
    tokens, blocks, width = queries.shape
    groups = width // kv_cache.shape[-1]
    fits = tokens == TILE and blocks == TILE and groups == TILE and lax.axis_size("ctx") == 2 * TILE
    chosen = chosen_body if fits else gathered_body
    return chosen(queries, kv_cache, page_counts, doc_ids)


def solution(mesh):
    placed = (
        P(("group", "ctx"), None, None),
        P(("group", "ctx"), None, None, None),
        P("group"),
        P("group"),
    )
    return jax.shard_map(
        body, mesh=mesh, in_specs=placed, out_specs=P(("group", "ctx"), None, None), check_vma=False
    )
```

```python
import functools
import math

import jax
import jax.numpy as jnp
from jax import lax
from jax.experimental import pallas as pl
from jax.experimental.pallas import tpu as pltpu
from jax.sharding import PartitionSpec as P

HEAD_DIM = 128
TILE = 8
STAT_ROWS = 16
VMEM_BYTES = 32 * 1024 * 1024


def doc_of(pages, doc_ends):
    return jnp.sum((pages[..., None] >= doc_ends).astype(jnp.int32), axis=-1)


def page_partial(rows, page_kv):
    tokens = rows.shape[0]
    kv_heads = page_kv.shape[-1] // HEAD_DIM
    groups = rows.shape[-1] // (kv_heads * HEAD_DIM)
    grouped = rows.reshape(tokens, kv_heads, groups, HEAD_DIM)
    keys = page_kv[0].reshape(-1, kv_heads, HEAD_DIM)
    values = page_kv[1].reshape(-1, kv_heads, HEAD_DIM)
    scores = jnp.einsum(
        "qhgd,khd->qhgk", grouped, keys, preferred_element_type=jnp.float32
    ) * HEAD_DIM ** (-0.5)
    row_max = jnp.max(scores, axis=-1)
    expo = jnp.exp(scores - row_max[..., None])
    row_sum = jnp.sum(expo, axis=-1)
    weights = expo.astype(jnp.bfloat16)
    mixed = jnp.einsum("qhgk,khd->qhgd", weights, values, preferred_element_type=jnp.float32)
    return (row_max.reshape(tokens, -1), row_sum.reshape(tokens, -1), mixed.reshape(tokens, -1))


def page_blocks(pages, page_counts, doc_ids):
    block_order = jnp.arange(doc_ids.shape[0], dtype=jnp.int32)
    page_docs = doc_of(pages, jnp.cumsum(page_counts))
    return jnp.sum(jnp.where(doc_ids == page_docs[:, None], block_order, 0), axis=-1)


def gathered_body(queries, kv_cache, page_counts, doc_ids):
    peers = lax.axis_size("ctx")
    local_rows, blocks, width = queries.shape
    heads = width // HEAD_DIM
    block_of = page_blocks(jnp.arange(peers, dtype=jnp.int32), page_counts, doc_ids)
    outgoing = jnp.take(queries, block_of, axis=1)
    arrived = lax.all_to_all(outgoing, "ctx", split_axis=1, concat_axis=0, tiled=True)
    row_max, row_sum, mixed = page_partial(arrived.reshape(-1, width), kv_cache[0])
    send = [part.reshape(peers, local_rows, -1) for part in (mixed, row_max, row_sum)]
    got_out, got_max, got_sum = [
        lax.all_to_all(part, "ctx", split_axis=0, concat_axis=0, tiled=True) for part in send
    ]
    matches = (block_of == jnp.arange(blocks, dtype=jnp.int32)[:, None])[..., None, None]
    masked = jnp.where(matches, got_max, -1e30)
    row_top = jnp.max(masked, axis=1, keepdims=True)
    weight = jnp.where(matches, jnp.exp(masked - row_top), 0.0)
    denominator = jnp.sum(weight * got_sum, axis=1)
    numerator = jnp.einsum(
        "cnrh,nrhd->crhd",
        weight,
        got_out.reshape(peers, local_rows, heads, HEAD_DIM),
        precision=lax.Precision.HIGHEST,
    )
    mixed_out = (numerator / denominator[..., None]).reshape(blocks, local_rows, width)
    return jnp.moveaxis(mixed_out, 0, 1).astype(jnp.bfloat16)


def pack_kernel(steps, listed, counts_hbm, ids_hbm, query_ref, *refs):
    count = len(steps)
    if listed:
        block_ref, *refs = refs
    sent_refs, (rows_ref, counts_ref, ids_ref, arrival, read) = refs[:count], refs[count:]
    small = [
        pltpu.make_async_copy(counts_hbm, counts_ref, read.at[0]),
        pltpu.make_async_copy(ids_hbm, ids_ref, read.at[1]),
    ]
    for copy in small:
        copy.start()
    tokens, blocks, width = query_ref.shape
    part = TILE * HEAD_DIM
    heads = range(width // part)
    spans = [slice(head * part, (head + 1) * part) for head in heads]
    copies = [
        pltpu.make_async_copy(query_ref.at[:, :, span], rows_ref.at[:, :, span], arrival.at[head])
        for head, span in zip(heads, spans)
    ]
    for copy in copies:
        copy.start()
    for copy in small:
        copy.wait()
    own = lax.axis_index("ctx")
    ends, end = [], 0
    for doc in range(blocks):
        end = end + counts_ref[doc]
        ends.append(end)
    ids = [ids_ref[block] for block in range(blocks)]
    asking = {}
    for step in listed or steps:
        page = own ^ step
        doc = sum((page >= end).astype(jnp.int32) for end in ends)
        block = sum(jnp.where(ids[c] == doc, c, 0) for c in range(1, blocks))
        if listed:
            block_ref[step] = block
        asking[step] = block
    row = lax.broadcasted_iota(jnp.int32, (tokens, tokens * blocks), 0)
    column = lax.broadcasted_iota(jnp.int32, (tokens, tokens * blocks), 1)
    pick = jnp.concatenate(
        [jnp.where(column == row * blocks + asking[step], 1.0, 0.0) for step in steps], axis=0
    ).astype(jnp.bfloat16)
    size = TILE * tokens
    for head in heads:
        copies[head].wait()
        rows = jnp.concatenate(
            [rows_ref[t, :, spans[head]].astype(jnp.float32) for t in range(tokens)], axis=0
        ).astype(jnp.bfloat16)
        picked = jnp.dot(pick, rows, preferred_element_type=jnp.float32)
        for n in range(count):
            own_rows = picked[n * tokens : (n + 1) * tokens]
            own_rows = jnp.concatenate(
                [own_rows[:, g * HEAD_DIM : (g + 1) * HEAD_DIM] for g in range(TILE)], axis=0
            )
            sent_refs[n][head * size : (head + 1) * size, :] = own_rows.astype(jnp.bfloat16)


def pack_queries(queries, page_counts, doc_ids, steps, listed):
    count = len(steps)
    tokens, _, width = queries.shape
    rows = tokens * width // HEAD_DIM
    vmem, smem = pl.BlockSpec(memory_space=pltpu.VMEM), pl.BlockSpec(memory_space=pltpu.SMEM)
    hbm = pl.BlockSpec(memory_space=pltpu.HBM)
    sent = pl.pallas_call(
        functools.partial(pack_kernel, steps, listed),
        out_shape=[jax.ShapeDtypeStruct((len(listed),), jnp.int32)] * bool(listed)
        + [jax.ShapeDtypeStruct((rows, HEAD_DIM), jnp.bfloat16)] * count,
        in_specs=[hbm, hbm, hbm],
        out_specs=[smem] * bool(listed) + [vmem] * count,
        scratch_shapes=[
            pltpu.VMEM(queries.shape, jnp.bfloat16),
            pltpu.SMEM(page_counts.shape, jnp.int32),
            pltpu.SMEM(doc_ids.shape, jnp.int32),
            pltpu.SemaphoreType.DMA((width // (TILE * HEAD_DIM),)),
            pltpu.SemaphoreType.DMA((2,)),
        ],
        cost_estimate=pl.CostEstimate(flops=0, bytes_accessed=1024, transcendentals=0),
        name="pack_queries",
    )(page_counts, doc_ids, queries)
    return sent


def attend_kernel(count, kv_ref, *refs):
    asked, answers, log_ref = refs[:count], refs[count : 2 * count], refs[2 * count]
    kv_heads = kv_ref.shape[2] // HEAD_DIM
    size = asked[0].shape[0] // kv_heads
    scale = HEAD_DIM ** (-0.5)

    for head in range(kv_heads):
        lanes = slice(head * HEAD_DIM, (head + 1) * HEAD_DIM)
        rows = slice(head * size, (head + 1) * size)
        query = jnp.concatenate([ref[rows, :] for ref in asked], axis=0)
        scores = lax.dot_general(
            kv_ref[0, :, lanes], query, (((1,), (1,)), ((), ())), preferred_element_type=jnp.float32
        )
        top = jnp.max(scores, axis=0, keepdims=True)
        expo = jnp.exp2((scores - top) * (scale / math.log(2.0)))
        total = jnp.sum(expo, axis=0, keepdims=True)
        mixed = lax.dot_general(
            expo.astype(jnp.bfloat16),
            kv_ref[1, :, lanes],
            (((0,), (0,)), ((), ())),
            preferred_element_type=jnp.float32,
        )
        mixed = mixed * jnp.transpose(jnp.broadcast_to(1.0 / total, (HEAD_DIM, total.shape[1])))
        for n in range(count):
            answers[n][rows, :] = mixed[n * size : (n + 1) * size].astype(jnp.bfloat16)
        log_ref[head : head + 1, :] = top * scale + jnp.log(total)
    logs = log_ref[...]
    high = logs.astype(jnp.bfloat16).astype(jnp.float32)
    middle = (logs - high).astype(jnp.bfloat16).astype(jnp.float32)
    low = logs - high - middle
    for n in range(count):
        span = slice(n * size, (n + 1) * size)
        upper = jnp.concatenate([high[:, span], middle[:, span]], axis=1)
        lower = jnp.concatenate([low[:, span], jnp.zeros_like(low[:, span])], axis=1)
        answers[n][kv_heads * size :, :] = jnp.concatenate([upper, lower], axis=0).astype(
            jnp.bfloat16
        )


def attend_page(page_kv, asked):
    count = len(asked)
    rows = asked[0].shape[0]
    kv_heads = page_kv.shape[2] // HEAD_DIM
    flops = 4 * count * rows * page_kv.shape[1] * HEAD_DIM
    return pl.pallas_call(
        functools.partial(attend_kernel, count),
        out_shape=[jax.ShapeDtypeStruct((rows + STAT_ROWS, HEAD_DIM), jnp.bfloat16)] * count,
        in_specs=[pl.BlockSpec(memory_space=pltpu.VMEM)] * (1 + count),
        out_specs=[pl.BlockSpec(memory_space=pltpu.VMEM)] * count,
        scratch_shapes=[pltpu.VMEM((kv_heads, count * rows // kv_heads), jnp.float32)],
        compiler_params=pltpu.CompilerParams(vmem_limit_bytes=VMEM_BYTES),
        cost_estimate=pl.CostEstimate(flops=0, bytes_accessed=1024, transcendentals=0),
        name="attend_page",
    )(page_kv, *asked)


def unpack_logs(part_ref, kv_heads):
    stat = part_ref[part_ref.shape[0] - STAT_ROWS :, :].astype(jnp.float32)
    size = stat.shape[1] // 2
    return stat[:kv_heads, :size] + stat[:kv_heads, size:] + stat[kv_heads:, :size]


def as_columns(shares):
    rows = jnp.concatenate(shares, axis=0)
    rows = jnp.concatenate([rows, jnp.zeros_like(rows)], axis=1)
    missing = HEAD_DIM - rows.shape[0] % HEAD_DIM
    if missing < HEAD_DIM:
        rows = jnp.concatenate([rows, jnp.zeros((missing, rows.shape[1]), jnp.float32)], axis=0)
    return jnp.transpose(rows)


def merge_kernel(steps, block_ref, *refs):
    count = len(steps)
    parts, (base_ref, top_ref, total_ref) = refs[:count], refs[count : count + 3]
    sum_refs = refs[count + 3 :]
    tokens, blocks, width = base_ref.shape
    size = TILE * tokens
    part = TILE * HEAD_DIM
    kv_heads = width // part
    top_ref[...] = jnp.full(top_ref.shape, -1e30, jnp.float32)
    total_ref[...] = jnp.zeros(total_ref.shape, jnp.float32)
    for sum_ref in sum_refs:
        sum_ref[...] = jnp.zeros(sum_ref.shape, jnp.float32)
    asking = [block_ref[step] for step in steps]
    logs = [unpack_logs(parts[n], kv_heads) for n in range(count)]
    for n in range(count):
        top_ref[asking[n]] = jnp.maximum(top_ref[asking[n]], logs[n])
    shares = [jnp.exp(logs[n] - top_ref[asking[n]]) for n in range(count)]
    for n in range(count):
        total_ref[asking[n]] += shares[n]
    columns = as_columns([shares[n] / total_ref[asking[n]] for n in range(count)])
    for n in range(count):
        for head, sum_ref in enumerate(sum_refs):
            place = n * kv_heads + head
            share = columns[:size, place : place + 1]
            part_rows = parts[n][head * size : (head + 1) * size, :]
            sum_ref[asking[n]] += share * part_rows.astype(jnp.float32)
    row = lax.broadcasted_iota(jnp.int32, (tokens * blocks, tokens * blocks), 0)
    column = lax.broadcasted_iota(jnp.int32, (tokens * blocks, tokens * blocks), 1)
    turned = (row // blocks == column % tokens) & (row % blocks == column // tokens)
    turn = jnp.where(turned, 1.0, 0.0).astype(jnp.bfloat16)
    for head, sum_ref in enumerate(sum_refs):
        span = slice(head * part, (head + 1) * part)
        lanes = [
            jnp.concatenate(
                [sum_ref[b, g * tokens : (g + 1) * tokens, :] for b in range(blocks)], axis=0
            )
            for g in range(TILE)
        ]
        block_rows = jnp.concatenate(lanes, axis=1).astype(jnp.bfloat16)
        token_rows = jnp.dot(turn, block_rows, preferred_element_type=jnp.float32)
        for t in range(tokens):
            base_ref[t, :, span] = token_rows[t * blocks : (t + 1) * blocks].astype(jnp.bfloat16)


def merge_pages(block_of, steps, parts, like):
    count = len(steps)
    tokens, blocks, width = like.shape
    kv_heads = width // (TILE * HEAD_DIM)
    size = TILE * tokens
    vmem = pl.BlockSpec(memory_space=pltpu.VMEM)
    stats = jax.ShapeDtypeStruct((blocks, kv_heads, size), jnp.float32)
    sums = jax.ShapeDtypeStruct((blocks, size, HEAD_DIM), jnp.float32)
    return pl.pallas_call(
        functools.partial(merge_kernel, steps),
        out_shape=[jax.ShapeDtypeStruct(like.shape, jnp.bfloat16), stats, stats]
        + [sums] * kv_heads,
        in_specs=[pl.BlockSpec(memory_space=pltpu.SMEM)] + [vmem] * count,
        out_specs=[vmem] * (3 + kv_heads),
        compiler_params=pltpu.CompilerParams(vmem_limit_bytes=VMEM_BYTES),
        cost_estimate=pl.CostEstimate(flops=0, bytes_accessed=1024, transcendentals=0),
        name="merge_pages",
    )(block_of, *[parts[step] for step in steps])


def settle_kernel(steps, block_ref, base_ref, top_ref, total_ref, *refs):
    count = len(steps)
    parts, sum_refs = refs[:count], refs[count:-3]
    out_ref, done_ref, leaving = refs[-3:]
    tokens, blocks, width = out_ref.shape
    size = TILE * tokens
    part = TILE * HEAD_DIM
    kv_heads = width // part
    asking = [block_ref[step] for step in steps]
    logs = [unpack_logs(ref, kv_heads) for ref in parts]
    shares = []
    for block in asking:
        old = top_ref[block]
        own = [jnp.where(asking[n] == block, logs[n], -1e30) for n in range(count)]
        top = functools.reduce(jnp.maximum, own, old)
        weights = [jnp.exp(old - top) * total_ref[block]] + [jnp.exp(log - top) for log in own]
        total = sum(weights)
        shares += [weight / total for weight in weights]
    columns = as_columns(shares)
    row = lax.broadcasted_iota(jnp.int32, (tokens * blocks, count * tokens), 0)
    column = lax.broadcasted_iota(jnp.int32, (tokens * blocks, count * tokens), 1)
    turned = jnp.zeros(row.shape, jnp.bool_)
    block_row = lax.broadcasted_iota(jnp.int32, (blocks, part), 0)
    fresh = jnp.zeros((blocks, part), jnp.bool_)
    for n, block in enumerate(asking):
        first = jnp.bool_(True)
        for m in range(n):
            first = first & (asking[m] != block)
        wanted = jnp.where(first, block, -1)
        turned = turned | (
            (row // blocks == column - n * tokens) & (row % blocks == wanted)
        )
        fresh = fresh | (block_row == block)
    turn = jnp.where(turned, 1.0, 0.0).astype(jnp.bfloat16)
    copies = []
    for head, sum_ref in enumerate(sum_refs):
        span = slice(head * part, (head + 1) * part)
        merged = []
        for n, block in enumerate(asking):
            rows = [sum_ref[block]]
            rows += [ref[head * size : (head + 1) * size, :].astype(jnp.float32) for ref in parts]
            total = None
            for m, value in enumerate(rows):
                place = (n * (count + 1) + m) * kv_heads + head
                term = columns[:size, place : place + 1] * value
                total = term if total is None else total + term
            merged.append(total)
        lanes = [
            jnp.concatenate([rows[g * tokens : (g + 1) * tokens, :] for rows in merged], axis=0)
            for g in range(TILE)
        ]
        block_rows = jnp.concatenate(lanes, axis=1).astype(jnp.bfloat16)
        token_rows = jnp.dot(turn, block_rows, preferred_element_type=jnp.float32)
        for t in range(tokens):
            new = token_rows[t * blocks : (t + 1) * blocks]
            old = base_ref[t, :, span].astype(jnp.float32)
            done_ref[t, :, span] = jnp.where(fresh, new, old).astype(jnp.bfloat16)
        copy = pltpu.make_async_copy(
            done_ref.at[:, :, span], out_ref.at[:, :, span], leaving.at[head]
        )
        copy.start()
        copies.append(copy)
    for copy in copies:
        copy.wait()


def settle_pages(block_of, merged, steps, parts):
    count = len(steps)
    base, top, total, *sums = merged
    vmem = pl.BlockSpec(memory_space=pltpu.VMEM)
    return pl.pallas_call(
        functools.partial(settle_kernel, steps),
        out_shape=jax.ShapeDtypeStruct(base.shape, jnp.bfloat16),
        in_specs=[pl.BlockSpec(memory_space=pltpu.SMEM)] + [vmem] * (3 + count + len(sums)),
        out_specs=pl.BlockSpec(memory_space=pltpu.HBM),
        scratch_shapes=[
            pltpu.VMEM(base.shape, jnp.bfloat16),
            pltpu.SemaphoreType.DMA((len(sums),)),
        ],
        compiler_params=pltpu.CompilerParams(vmem_limit_bytes=VMEM_BYTES),
        cost_estimate=pl.CostEstimate(flops=0, bytes_accessed=1024, transcendentals=0),
        name="settle_pages",
    )(block_of, base, top, total, *[parts[step] for step in steps], *sums)


class Window:
    def __init__(self, far, depth):
        self.far, self.depth = far, depth
        self.arrived = {False: [], True: []}

    def swap(self, value, step):
        if step == 0:
            return value
        arrived = self.arrived[step >= self.far]
        if len(arrived) >= self.depth:
            value, _ = lax.optimization_barrier((value, arrived[-self.depth]))
        count = lax.axis_size("ctx")
        pairs = [(source, source ^ step) for source in range(count)]
        arrived.append(lax.ppermute(value, "ctx", pairs))
        return arrived[-1]


def stepped_body(queries, kv_cache, page_counts, doc_ids):
    every = tuple(range(lax.axis_size("ctx")))
    early = (8, 9)
    late = tuple(step for step in every if step not in early)
    first = pack_queries(queries, page_counts, doc_ids, early, ())
    block_of, *rest = pack_queries(queries, page_counts, doc_ids, late, every)
    sent = dict(zip(early + late, [*first, *rest]))
    window = Window(len(every) // 2, 3)
    asked, parts = {}, {}

    def ask(*steps):
        for step in steps:
            asked[step] = window.swap(sent[step], step)

    def attend(*steps):
        for step, part in zip(steps, attend_page(kv_cache[0], [asked[s] for s in steps])):
            parts[step] = part

    def answer(*steps):
        for step in steps:
            parts[step] = window.swap(parts[step], step)

    ask(8, 9, 1, 10, 11, 2, 4, 12, 13, 3, 14, 5, 15, 6, 7, 0)
    attend(0, 1, 2, 3)
    attend(8, 9, 10, 11)
    answer(8, 9, 1, 10, 2)
    attend(4, 5, 6, 7)
    answer(11, 4, 3)
    attend(12, 13, 14, 15)
    answer(12, 5, 13, 6, 14, 7, 15)
    last = (7, 15)
    before = tuple(step for step in every if step not in last)
    merged = merge_pages(block_of, before, parts, queries)
    return settle_pages(block_of, merged, last, parts)


def body(queries, kv_cache, page_counts, doc_ids):
    tokens, blocks, width = queries.shape
    groups = width // kv_cache.shape[-1]
    fits = tokens == TILE and blocks == TILE and groups == TILE and lax.axis_size("ctx") == 2 * TILE
    chosen = stepped_body if fits else gathered_body
    return chosen(queries, kv_cache, page_counts, doc_ids)


def solution(mesh):
    placed = (
        P(("group", "ctx"), None, None),
        P(("group", "ctx"), None, None, None),
        P("group"),
        P("group"),
    )
    return jax.shard_map(
        body, mesh=mesh, in_specs=placed, out_specs=P(("group", "ctx"), None, None), check_vma=False
    )
```

```python
import functools
import math

import jax
import jax.numpy as jnp
from jax import lax
from jax.experimental import pallas as pl
from jax.experimental.pallas import tpu as pltpu
from jax.sharding import PartitionSpec as P

HEAD_DIM = 128
TILE = 8
STAT_ROWS = 16
VMEM_BYTES = 32 * 1024 * 1024


def doc_of(pages, doc_ends):
    return jnp.sum((pages[..., None] >= doc_ends).astype(jnp.int32), axis=-1)


def page_partial(rows, page_kv):
    tokens = rows.shape[0]
    kv_heads = page_kv.shape[-1] // HEAD_DIM
    groups = rows.shape[-1] // (kv_heads * HEAD_DIM)
    grouped = rows.reshape(tokens, kv_heads, groups, HEAD_DIM)
    keys = page_kv[0].reshape(-1, kv_heads, HEAD_DIM)
    values = page_kv[1].reshape(-1, kv_heads, HEAD_DIM)
    scores = jnp.einsum(
        "qhgd,khd->qhgk", grouped, keys, preferred_element_type=jnp.float32
    ) * HEAD_DIM ** (-0.5)
    row_max = jnp.max(scores, axis=-1)
    expo = jnp.exp(scores - row_max[..., None])
    row_sum = jnp.sum(expo, axis=-1)
    weights = expo.astype(jnp.bfloat16)
    mixed = jnp.einsum("qhgk,khd->qhgd", weights, values, preferred_element_type=jnp.float32)
    return (row_max.reshape(tokens, -1), row_sum.reshape(tokens, -1), mixed.reshape(tokens, -1))


def page_blocks(pages, page_counts, doc_ids):
    block_order = jnp.arange(doc_ids.shape[0], dtype=jnp.int32)
    page_docs = doc_of(pages, jnp.cumsum(page_counts))
    return jnp.sum(jnp.where(doc_ids == page_docs[:, None], block_order, 0), axis=-1)


def gathered_body(queries, kv_cache, page_counts, doc_ids):
    peers = lax.axis_size("ctx")
    local_rows, blocks, width = queries.shape
    heads = width // HEAD_DIM
    block_of = page_blocks(jnp.arange(peers, dtype=jnp.int32), page_counts, doc_ids)
    outgoing = jnp.take(queries, block_of, axis=1)
    arrived = lax.all_to_all(outgoing, "ctx", split_axis=1, concat_axis=0, tiled=True)
    row_max, row_sum, mixed = page_partial(arrived.reshape(-1, width), kv_cache[0])
    send = [part.reshape(peers, local_rows, -1) for part in (mixed, row_max, row_sum)]
    got_out, got_max, got_sum = [
        lax.all_to_all(part, "ctx", split_axis=0, concat_axis=0, tiled=True) for part in send
    ]
    matches = (block_of == jnp.arange(blocks, dtype=jnp.int32)[:, None])[..., None, None]
    masked = jnp.where(matches, got_max, -1e30)
    row_top = jnp.max(masked, axis=1, keepdims=True)
    weight = jnp.where(matches, jnp.exp(masked - row_top), 0.0)
    denominator = jnp.sum(weight * got_sum, axis=1)
    numerator = jnp.einsum(
        "cnrh,nrhd->crhd",
        weight,
        got_out.reshape(peers, local_rows, heads, HEAD_DIM),
        precision=lax.Precision.HIGHEST,
    )
    mixed_out = (numerator / denominator[..., None]).reshape(blocks, local_rows, width)
    return jnp.moveaxis(mixed_out, 0, 1).astype(jnp.bfloat16)


def pack_kernel(steps, listed, counts_hbm, ids_hbm, query_ref, block_ref, *refs):
    count = len(steps)
    sent_refs, (rows_ref, counts_ref, ids_ref, arrival, read) = refs[:count], refs[count:]
    small = [
        pltpu.make_async_copy(counts_hbm, counts_ref, read.at[0]),
        pltpu.make_async_copy(ids_hbm, ids_ref, read.at[1]),
    ]
    for copy in small:
        copy.start()
    tokens, blocks, width = query_ref.shape
    part = TILE * HEAD_DIM
    heads = range(width // part)
    spans = [slice(head * part, (head + 1) * part) for head in heads]
    copies = [
        pltpu.make_async_copy(query_ref.at[:, :, span], rows_ref.at[:, :, span], arrival.at[head])
        for head, span in zip(heads, spans)
    ]
    for copy in copies:
        copy.start()
    for copy in small:
        copy.wait()
    own = lax.axis_index("ctx")
    ends, end = [], 0
    for doc in range(blocks):
        end = end + counts_ref[doc]
        ends.append(end)
    ids = [ids_ref[block] for block in range(blocks)]
    asking = {}
    for n, step in enumerate(listed):
        page = own ^ step
        doc = sum((page >= end).astype(jnp.int32) for end in ends)
        block = sum(jnp.where(ids[c] == doc, c, 0) for c in range(1, blocks))
        block_ref[n] = block
        asking[step] = block
    row = lax.broadcasted_iota(jnp.int32, (tokens, tokens * blocks), 0)
    column = lax.broadcasted_iota(jnp.int32, (tokens, tokens * blocks), 1)
    pick = jnp.concatenate(
        [jnp.where(column == row * blocks + asking[step], 1.0, 0.0) for step in steps], axis=0
    ).astype(jnp.bfloat16)
    size = TILE * tokens
    for head in heads:
        copies[head].wait()
        rows = jnp.concatenate(
            [rows_ref[t, :, spans[head]].astype(jnp.float32) for t in range(tokens)], axis=0
        ).astype(jnp.bfloat16)
        picked = jnp.dot(pick, rows, preferred_element_type=jnp.float32)
        for n in range(count):
            own_rows = picked[n * tokens : (n + 1) * tokens]
            own_rows = jnp.concatenate(
                [own_rows[:, g * HEAD_DIM : (g + 1) * HEAD_DIM] for g in range(TILE)], axis=0
            )
            sent_refs[n][head * size : (head + 1) * size, :] = own_rows.astype(jnp.bfloat16)


def pack_queries(queries, page_counts, doc_ids, steps, listed):
    count = len(steps)
    tokens, _, width = queries.shape
    rows = tokens * width // HEAD_DIM
    vmem, smem = pl.BlockSpec(memory_space=pltpu.VMEM), pl.BlockSpec(memory_space=pltpu.SMEM)
    hbm = pl.BlockSpec(memory_space=pltpu.HBM)
    block_of, *sent = pl.pallas_call(
        functools.partial(pack_kernel, steps, listed),
        out_shape=[jax.ShapeDtypeStruct((len(listed),), jnp.int32)]
        + [jax.ShapeDtypeStruct((rows, HEAD_DIM), jnp.bfloat16)] * count,
        in_specs=[hbm, hbm, hbm],
        out_specs=[smem] + [vmem] * count,
        scratch_shapes=[
            pltpu.VMEM(queries.shape, jnp.bfloat16),
            pltpu.SMEM(page_counts.shape, jnp.int32),
            pltpu.SMEM(doc_ids.shape, jnp.int32),
            pltpu.SemaphoreType.DMA((width // (TILE * HEAD_DIM),)),
            pltpu.SemaphoreType.DMA((2,)),
        ],
        cost_estimate=pl.CostEstimate(flops=0, bytes_accessed=4 << 20, transcendentals=0),
        name="pack_queries",
    )(page_counts, doc_ids, queries)
    return block_of, sent


def attend_kernel(count, kv_ref, *refs):
    asked, answers, log_ref = refs[:count], refs[count : 2 * count], refs[2 * count]
    kv_heads = kv_ref.shape[2] // HEAD_DIM
    size = asked[0].shape[0] // kv_heads
    scale = HEAD_DIM ** (-0.5)

    for head in range(kv_heads):
        lanes = slice(head * HEAD_DIM, (head + 1) * HEAD_DIM)
        rows = slice(head * size, (head + 1) * size)
        query = jnp.concatenate([ref[rows, :] for ref in asked], axis=0)
        scores = lax.dot_general(
            kv_ref[0, :, lanes], query, (((1,), (1,)), ((), ())), preferred_element_type=jnp.float32
        )
        top = jnp.max(scores, axis=0, keepdims=True)
        expo = jnp.exp2((scores - top) * (scale / math.log(2.0)))
        total = jnp.sum(expo, axis=0, keepdims=True)
        mixed = lax.dot_general(
            expo.astype(jnp.bfloat16),
            kv_ref[1, :, lanes],
            (((0,), (0,)), ((), ())),
            preferred_element_type=jnp.float32,
        )
        mixed = mixed * jnp.transpose(jnp.broadcast_to(1.0 / total, (HEAD_DIM, total.shape[1])))
        for n in range(count):
            answers[n][rows, :] = mixed[n * size : (n + 1) * size].astype(jnp.bfloat16)
        log_ref[head : head + 1, :] = top * scale + jnp.log(total)
    logs = log_ref[...]
    high = logs.astype(jnp.bfloat16).astype(jnp.float32)
    middle = (logs - high).astype(jnp.bfloat16).astype(jnp.float32)
    low = logs - high - middle
    for n in range(count):
        span = slice(n * size, (n + 1) * size)
        upper = jnp.concatenate([high[:, span], middle[:, span]], axis=1)
        lower = jnp.concatenate([low[:, span], jnp.zeros_like(low[:, span])], axis=1)
        answers[n][kv_heads * size :, :] = jnp.concatenate([upper, lower], axis=0).astype(
            jnp.bfloat16
        )


def attend_page(page_kv, asked):
    count = len(asked)
    rows = asked[0].shape[0]
    kv_heads = page_kv.shape[2] // HEAD_DIM
    flops = 4 * count * rows * page_kv.shape[1] * HEAD_DIM
    return pl.pallas_call(
        functools.partial(attend_kernel, count),
        out_shape=[jax.ShapeDtypeStruct((rows + STAT_ROWS, HEAD_DIM), jnp.bfloat16)] * count,
        in_specs=[pl.BlockSpec(memory_space=pltpu.VMEM)] * (1 + count),
        out_specs=[pl.BlockSpec(memory_space=pltpu.VMEM)] * count,
        scratch_shapes=[pltpu.VMEM((kv_heads, count * rows // kv_heads), jnp.float32)],
        compiler_params=pltpu.CompilerParams(vmem_limit_bytes=VMEM_BYTES),
        cost_estimate=pl.CostEstimate(
            flops=flops, bytes_accessed=3 << 20, transcendentals=flops // 512
        ),
        name="attend_page",
    )(page_kv, *asked)


def unpack_logs(part_ref, kv_heads):
    stat = part_ref[part_ref.shape[0] - STAT_ROWS :, :].astype(jnp.float32)
    size = stat.shape[1] // 2
    return stat[:kv_heads, :size] + stat[:kv_heads, size:] + stat[kv_heads:, :size]


def as_columns(shares):
    rows = jnp.concatenate(shares, axis=0)
    rows = jnp.concatenate([rows, jnp.zeros_like(rows)], axis=1)
    missing = HEAD_DIM - rows.shape[0] % HEAD_DIM
    if missing < HEAD_DIM:
        rows = jnp.concatenate([rows, jnp.zeros((missing, rows.shape[1]), jnp.float32)], axis=0)
    return jnp.transpose(rows)


def merge_kernel(steps, block_ref, *refs):
    count = len(steps)
    parts, (base_ref, top_ref, total_ref) = refs[:count], refs[count : count + 3]
    sum_refs = refs[count + 3 :]
    tokens, blocks, width = base_ref.shape
    size = TILE * tokens
    part = TILE * HEAD_DIM
    kv_heads = width // part
    top_ref[...] = jnp.full(top_ref.shape, -1e30, jnp.float32)
    total_ref[...] = jnp.zeros(total_ref.shape, jnp.float32)
    for sum_ref in sum_refs:
        sum_ref[...] = jnp.zeros(sum_ref.shape, jnp.float32)
    asking = [block_ref[step] for step in steps]
    logs = [unpack_logs(parts[n], kv_heads) for n in range(count)]
    for n in range(count):
        top_ref[asking[n]] = jnp.maximum(top_ref[asking[n]], logs[n])
    shares = [jnp.exp(logs[n] - top_ref[asking[n]]) for n in range(count)]
    for n in range(count):
        total_ref[asking[n]] += shares[n]
    columns = as_columns([shares[n] / total_ref[asking[n]] for n in range(count)])
    for n in range(count):
        for head, sum_ref in enumerate(sum_refs):
            place = n * kv_heads + head
            share = columns[:size, place : place + 1]
            part_rows = parts[n][head * size : (head + 1) * size, :]
            sum_ref[asking[n]] += share * part_rows.astype(jnp.float32)
    row = lax.broadcasted_iota(jnp.int32, (tokens * blocks, tokens * blocks), 0)
    column = lax.broadcasted_iota(jnp.int32, (tokens * blocks, tokens * blocks), 1)
    turned = (row // blocks == column % tokens) & (row % blocks == column // tokens)
    turn = jnp.where(turned, 1.0, 0.0).astype(jnp.bfloat16)
    for head, sum_ref in enumerate(sum_refs):
        span = slice(head * part, (head + 1) * part)
        lanes = [
            jnp.concatenate(
                [sum_ref[b, g * tokens : (g + 1) * tokens, :] for b in range(blocks)], axis=0
            )
            for g in range(TILE)
        ]
        block_rows = jnp.concatenate(lanes, axis=1).astype(jnp.bfloat16)
        token_rows = jnp.dot(turn, block_rows, preferred_element_type=jnp.float32)
        for t in range(tokens):
            base_ref[t, :, span] = token_rows[t * blocks : (t + 1) * blocks].astype(jnp.bfloat16)


def merge_pages(block_of, steps, parts, like):
    count = len(steps)
    tokens, blocks, width = like.shape
    kv_heads = width // (TILE * HEAD_DIM)
    size = TILE * tokens
    vmem = pl.BlockSpec(memory_space=pltpu.VMEM)
    stats = jax.ShapeDtypeStruct((blocks, kv_heads, size), jnp.float32)
    sums = jax.ShapeDtypeStruct((blocks, size, HEAD_DIM), jnp.float32)
    return pl.pallas_call(
        functools.partial(merge_kernel, steps),
        out_shape=[jax.ShapeDtypeStruct(like.shape, jnp.bfloat16), stats, stats]
        + [sums] * kv_heads,
        in_specs=[pl.BlockSpec(memory_space=pltpu.SMEM)] + [vmem] * count,
        out_specs=[vmem] * (3 + kv_heads),
        compiler_params=pltpu.CompilerParams(vmem_limit_bytes=VMEM_BYTES),
        cost_estimate=pl.CostEstimate(flops=0, bytes_accessed=4 << 20, transcendentals=0),
        name="merge_pages",
    )(block_of, *[parts[step] for step in steps])


def settle_kernel(steps, block_ref, base_ref, top_ref, total_ref, *refs):
    count = len(steps)
    parts, sum_refs = refs[:count], refs[count:-3]
    out_ref, done_ref, leaving = refs[-3:]
    tokens, blocks, width = out_ref.shape
    size = TILE * tokens
    part = TILE * HEAD_DIM
    kv_heads = width // part
    asking = [block_ref[step] for step in steps]
    logs = [unpack_logs(ref, kv_heads) for ref in parts]
    shares = []
    for block in asking:
        old = top_ref[block]
        own = [jnp.where(asking[n] == block, logs[n], -1e30) for n in range(count)]
        top = functools.reduce(jnp.maximum, own, old)
        weights = [jnp.exp(old - top) * total_ref[block]] + [jnp.exp(log - top) for log in own]
        total = sum(weights)
        shares += [weight / total for weight in weights]
    columns = as_columns(shares)
    row = lax.broadcasted_iota(jnp.int32, (tokens * blocks, count * tokens), 0)
    column = lax.broadcasted_iota(jnp.int32, (tokens * blocks, count * tokens), 1)
    turned = jnp.zeros(row.shape, jnp.bool_)
    block_row = lax.broadcasted_iota(jnp.int32, (blocks, part), 0)
    fresh = jnp.zeros((blocks, part), jnp.bool_)
    for n, block in enumerate(asking):
        first = jnp.bool_(True)
        for m in range(n):
            first = first & (asking[m] != block)
        wanted = jnp.where(first, block, -1)
        turned = turned | (
            (row // blocks == column - n * tokens) & (row % blocks == wanted)
        )
        fresh = fresh | (block_row == block)
    turn = jnp.where(turned, 1.0, 0.0).astype(jnp.bfloat16)
    copies = []
    for head, sum_ref in enumerate(sum_refs):
        span = slice(head * part, (head + 1) * part)
        merged = []
        for n, block in enumerate(asking):
            rows = [sum_ref[block]]
            rows += [ref[head * size : (head + 1) * size, :].astype(jnp.float32) for ref in parts]
            total = None
            for m, value in enumerate(rows):
                place = (n * (count + 1) + m) * kv_heads + head
                term = columns[:size, place : place + 1] * value
                total = term if total is None else total + term
            merged.append(total)
        lanes = [
            jnp.concatenate([rows[g * tokens : (g + 1) * tokens, :] for rows in merged], axis=0)
            for g in range(TILE)
        ]
        block_rows = jnp.concatenate(lanes, axis=1).astype(jnp.bfloat16)
        token_rows = jnp.dot(turn, block_rows, preferred_element_type=jnp.float32)
        for t in range(tokens):
            new = token_rows[t * blocks : (t + 1) * blocks]
            old = base_ref[t, :, span].astype(jnp.float32)
            done_ref[t, :, span] = jnp.where(fresh, new, old).astype(jnp.bfloat16)
        copy = pltpu.make_async_copy(
            done_ref.at[:, :, span], out_ref.at[:, :, span], leaving.at[head]
        )
        copy.start()
        copies.append(copy)
    for copy in copies:
        copy.wait()


def settle_pages(block_of, merged, steps, parts):
    count = len(steps)
    base, top, total, *sums = merged
    vmem = pl.BlockSpec(memory_space=pltpu.VMEM)
    return pl.pallas_call(
        functools.partial(settle_kernel, steps),
        out_shape=jax.ShapeDtypeStruct(base.shape, jnp.bfloat16),
        in_specs=[pl.BlockSpec(memory_space=pltpu.SMEM)] + [vmem] * (3 + count + len(sums)),
        out_specs=pl.BlockSpec(memory_space=pltpu.HBM),
        scratch_shapes=[
            pltpu.VMEM(base.shape, jnp.bfloat16),
            pltpu.SemaphoreType.DMA((len(sums),)),
        ],
        compiler_params=pltpu.CompilerParams(vmem_limit_bytes=VMEM_BYTES),
        cost_estimate=pl.CostEstimate(flops=0, bytes_accessed=4 << 20, transcendentals=0),
        name="settle_pages",
    )(block_of, base, top, total, *[parts[step] for step in steps], *sums)


class Window:
    def __init__(self, far, depth):
        self.far, self.depth = far, depth
        self.arrived = {False: [], True: []}

    def swap(self, value, step):
        if step == 0:
            return value
        arrived = self.arrived[step >= self.far]
        if len(arrived) >= self.depth:
            value, _ = lax.optimization_barrier((value, arrived[-self.depth]))
        count = lax.axis_size("ctx")
        pairs = [(source, source ^ step) for source in range(count)]
        arrived.append(lax.ppermute(value, "ctx", pairs))
        return arrived[-1]


def stepped_body(queries, kv_cache, page_counts, doc_ids):
    every = tuple(range(lax.axis_size("ctx")))
    early = (8, 9)
    late = tuple(step for step in every if step not in early)
    _, first = pack_queries(queries, page_counts, doc_ids, early, early)
    block_of, rest = pack_queries(queries, page_counts, doc_ids, late, every)
    sent = dict(zip(early + late, first + rest))
    window = Window(len(every) // 2, 3)
    asked, parts = {}, {}

    def ask(*steps):
        for step in steps:
            asked[step] = window.swap(sent[step], step)

    def attend(*steps):
        for step, part in zip(steps, attend_page(kv_cache[0], [asked[s] for s in steps])):
            parts[step] = part

    def answer(*steps):
        for step in steps:
            parts[step] = window.swap(parts[step], step)

    ask(8, 9, 1, 10, 11, 2, 4, 12, 13, 3, 14, 5, 15, 6, 7, 0)
    attend(0, 1, 2, 3)
    attend(8, 9, 10, 11)
    answer(8, 9, 1, 10, 2)
    attend(4, 5, 6, 7)
    answer(11, 4, 3)
    attend(12, 13, 14, 15)
    answer(12, 5, 13, 6, 7, 14, 15)
    last = (15,)
    before = tuple(step for step in every if step not in last)
    merged = merge_pages(block_of, before, parts, queries)
    return settle_pages(block_of, merged, last, parts)


def body(queries, kv_cache, page_counts, doc_ids):
    tokens, blocks, width = queries.shape
    groups = width // kv_cache.shape[-1]
    fits = tokens == TILE and blocks == TILE and groups == TILE and lax.axis_size("ctx") == 2 * TILE
    chosen = stepped_body if fits else gathered_body
    return chosen(queries, kv_cache, page_counts, doc_ids)


def solution(mesh):
    placed = (
        P(("group", "ctx"), None, None),
        P(("group", "ctx"), None, None, None),
        P("group"),
        P("group"),
    )
    return jax.shard_map(
        body, mesh=mesh, in_specs=placed, out_specs=P(("group", "ctx"), None, None), check_vma=False
    )
```

```python
import functools
import math

import jax
import jax.numpy as jnp
from jax import lax
from jax.experimental import pallas as pl
from jax.experimental.pallas import tpu as pltpu
from jax.sharding import PartitionSpec as P

HEAD_DIM = 128
TILE = 8
STAT_ROWS = 16
VMEM_BYTES = 32 * 1024 * 1024


def doc_of(pages, doc_ends):
    return jnp.sum((pages[..., None] >= doc_ends).astype(jnp.int32), axis=-1)


def page_partial(rows, page_kv):
    tokens = rows.shape[0]
    kv_heads = page_kv.shape[-1] // HEAD_DIM
    groups = rows.shape[-1] // (kv_heads * HEAD_DIM)
    grouped = rows.reshape(tokens, kv_heads, groups, HEAD_DIM)
    keys = page_kv[0].reshape(-1, kv_heads, HEAD_DIM)
    values = page_kv[1].reshape(-1, kv_heads, HEAD_DIM)
    scores = jnp.einsum(
        "qhgd,khd->qhgk", grouped, keys, preferred_element_type=jnp.float32
    ) * HEAD_DIM ** (-0.5)
    row_max = jnp.max(scores, axis=-1)
    expo = jnp.exp(scores - row_max[..., None])
    row_sum = jnp.sum(expo, axis=-1)
    weights = expo.astype(jnp.bfloat16)
    mixed = jnp.einsum("qhgk,khd->qhgd", weights, values, preferred_element_type=jnp.float32)
    return (row_max.reshape(tokens, -1), row_sum.reshape(tokens, -1), mixed.reshape(tokens, -1))


def page_blocks(pages, page_counts, doc_ids):
    block_order = jnp.arange(doc_ids.shape[0], dtype=jnp.int32)
    page_docs = doc_of(pages, jnp.cumsum(page_counts))
    return jnp.sum(jnp.where(doc_ids == page_docs[:, None], block_order, 0), axis=-1)


def gathered_body(queries, kv_cache, page_counts, doc_ids):
    peers = lax.axis_size("ctx")
    local_rows, blocks, width = queries.shape
    heads = width // HEAD_DIM
    block_of = page_blocks(jnp.arange(peers, dtype=jnp.int32), page_counts, doc_ids)
    outgoing = jnp.take(queries, block_of, axis=1)
    arrived = lax.all_to_all(outgoing, "ctx", split_axis=1, concat_axis=0, tiled=True)
    row_max, row_sum, mixed = page_partial(arrived.reshape(-1, width), kv_cache[0])
    send = [part.reshape(peers, local_rows, -1) for part in (mixed, row_max, row_sum)]
    got_out, got_max, got_sum = [
        lax.all_to_all(part, "ctx", split_axis=0, concat_axis=0, tiled=True) for part in send
    ]
    matches = (block_of == jnp.arange(blocks, dtype=jnp.int32)[:, None])[..., None, None]
    masked = jnp.where(matches, got_max, -1e30)
    row_top = jnp.max(masked, axis=1, keepdims=True)
    weight = jnp.where(matches, jnp.exp(masked - row_top), 0.0)
    denominator = jnp.sum(weight * got_sum, axis=1)
    numerator = jnp.einsum(
        "cnrh,nrhd->crhd",
        weight,
        got_out.reshape(peers, local_rows, heads, HEAD_DIM),
        precision=lax.Precision.HIGHEST,
    )
    mixed_out = (numerator / denominator[..., None]).reshape(blocks, local_rows, width)
    return jnp.moveaxis(mixed_out, 0, 1).astype(jnp.bfloat16)


def pack_kernel(steps, listed, counts_hbm, ids_hbm, query_ref, block_ref, *refs):
    count = len(steps)
    sent_refs, (rows_ref, counts_ref, ids_ref, arrival, read) = refs[:count], refs[count:]
    small = [
        pltpu.make_async_copy(counts_hbm, counts_ref, read.at[0]),
        pltpu.make_async_copy(ids_hbm, ids_ref, read.at[1]),
    ]
    for copy in small:
        copy.start()
    tokens, blocks, width = query_ref.shape
    part = TILE * HEAD_DIM
    heads = range(width // part)
    spans = [slice(head * part, (head + 1) * part) for head in heads]
    copies = [
        pltpu.make_async_copy(query_ref.at[:, :, span], rows_ref.at[:, :, span], arrival.at[head])
        for head, span in zip(heads, spans)
    ]
    for copy in copies:
        copy.start()
    for copy in small:
        copy.wait()
    own = lax.axis_index("ctx")
    ends, end = [], 0
    for doc in range(blocks):
        end = end + counts_ref[doc]
        ends.append(end)
    ids = [ids_ref[block] for block in range(blocks)]
    asking = {}
    for n, step in enumerate(listed):
        page = own ^ step
        doc = sum((page >= end).astype(jnp.int32) for end in ends)
        block = sum(jnp.where(ids[c] == doc, c, 0) for c in range(1, blocks))
        block_ref[n] = block
        asking[step] = block
    row = lax.broadcasted_iota(jnp.int32, (tokens, tokens * blocks), 0)
    column = lax.broadcasted_iota(jnp.int32, (tokens, tokens * blocks), 1)
    pick = jnp.concatenate(
        [jnp.where(column == row * blocks + asking[step], 1.0, 0.0) for step in steps], axis=0
    ).astype(jnp.bfloat16)
    size = TILE * tokens
    for head in heads:
        copies[head].wait()
        rows = jnp.concatenate(
            [rows_ref[t, :, spans[head]].astype(jnp.float32) for t in range(tokens)], axis=0
        ).astype(jnp.bfloat16)
        picked = jnp.dot(pick, rows, preferred_element_type=jnp.float32)
        for n in range(count):
            own_rows = picked[n * tokens : (n + 1) * tokens]
            own_rows = jnp.concatenate(
                [own_rows[:, g * HEAD_DIM : (g + 1) * HEAD_DIM] for g in range(TILE)], axis=0
            )
            sent_refs[n][head * size : (head + 1) * size, :] = own_rows.astype(jnp.bfloat16)


def pack_queries(queries, page_counts, doc_ids, steps, listed):
    count = len(steps)
    tokens, _, width = queries.shape
    rows = tokens * width // HEAD_DIM
    vmem, smem = pl.BlockSpec(memory_space=pltpu.VMEM), pl.BlockSpec(memory_space=pltpu.SMEM)
    hbm = pl.BlockSpec(memory_space=pltpu.HBM)
    block_of, *sent = pl.pallas_call(
        functools.partial(pack_kernel, steps, listed),
        out_shape=[jax.ShapeDtypeStruct((len(listed),), jnp.int32)]
        + [jax.ShapeDtypeStruct((rows, HEAD_DIM), jnp.bfloat16)] * count,
        in_specs=[hbm, hbm, hbm],
        out_specs=[smem] + [vmem] * count,
        scratch_shapes=[
            pltpu.VMEM(queries.shape, jnp.bfloat16),
            pltpu.SMEM(page_counts.shape, jnp.int32),
            pltpu.SMEM(doc_ids.shape, jnp.int32),
            pltpu.SemaphoreType.DMA((width // (TILE * HEAD_DIM),)),
            pltpu.SemaphoreType.DMA((2,)),
        ],
        cost_estimate=pl.CostEstimate(flops=0, bytes_accessed=4 << 20, transcendentals=0),
        name="pack_queries",
    )(page_counts, doc_ids, queries)
    return block_of, sent


def attend_kernel(count, kv_ref, *refs):
    asked, answers, log_ref = refs[:count], refs[count : 2 * count], refs[2 * count]
    kv_heads = kv_ref.shape[2] // HEAD_DIM
    size = asked[0].shape[0] // kv_heads
    scale = HEAD_DIM ** (-0.5)

    for head in range(kv_heads):
        lanes = slice(head * HEAD_DIM, (head + 1) * HEAD_DIM)
        rows = slice(head * size, (head + 1) * size)
        query = jnp.concatenate([ref[rows, :] for ref in asked], axis=0)
        scores = lax.dot_general(
            kv_ref[0, :, lanes], query, (((1,), (1,)), ((), ())), preferred_element_type=jnp.float32
        )
        top = jnp.max(scores, axis=0, keepdims=True)
        expo = jnp.exp2((scores - top) * (scale / math.log(2.0)))
        total = jnp.sum(expo, axis=0, keepdims=True)
        mixed = lax.dot_general(
            expo.astype(jnp.bfloat16),
            kv_ref[1, :, lanes],
            (((0,), (0,)), ((), ())),
            preferred_element_type=jnp.float32,
        )
        mixed = mixed * jnp.transpose(jnp.broadcast_to(1.0 / total, (HEAD_DIM, total.shape[1])))
        for n in range(count):
            answers[n][rows, :] = mixed[n * size : (n + 1) * size].astype(jnp.bfloat16)
        log_ref[head : head + 1, :] = top * scale + jnp.log(total)
    logs = log_ref[...]
    high = logs.astype(jnp.bfloat16).astype(jnp.float32)
    middle = (logs - high).astype(jnp.bfloat16).astype(jnp.float32)
    low = logs - high - middle
    for n in range(count):
        span = slice(n * size, (n + 1) * size)
        upper = jnp.concatenate([high[:, span], middle[:, span]], axis=1)
        lower = jnp.concatenate([low[:, span], jnp.zeros_like(low[:, span])], axis=1)
        answers[n][kv_heads * size :, :] = jnp.concatenate([upper, lower], axis=0).astype(
            jnp.bfloat16
        )


def attend_page(page_kv, asked):
    count = len(asked)
    rows = asked[0].shape[0]
    kv_heads = page_kv.shape[2] // HEAD_DIM
    flops = 4 * count * rows * page_kv.shape[1] * HEAD_DIM
    return pl.pallas_call(
        functools.partial(attend_kernel, count),
        out_shape=[jax.ShapeDtypeStruct((rows + STAT_ROWS, HEAD_DIM), jnp.bfloat16)] * count,
        in_specs=[pl.BlockSpec(memory_space=pltpu.VMEM)] * (1 + count),
        out_specs=[pl.BlockSpec(memory_space=pltpu.VMEM)] * count,
        scratch_shapes=[pltpu.VMEM((kv_heads, count * rows // kv_heads), jnp.float32)],
        compiler_params=pltpu.CompilerParams(vmem_limit_bytes=VMEM_BYTES),
        cost_estimate=pl.CostEstimate(
            flops=flops, bytes_accessed=3 << 20, transcendentals=flops // 512
        ),
        name="attend_page",
    )(page_kv, *asked)


def unpack_logs(part_ref, kv_heads):
    stat = part_ref[part_ref.shape[0] - STAT_ROWS :, :].astype(jnp.float32)
    size = stat.shape[1] // 2
    return stat[:kv_heads, :size] + stat[:kv_heads, size:] + stat[kv_heads:, :size]


def as_columns(shares):
    rows = jnp.concatenate(shares, axis=0)
    rows = jnp.concatenate([rows, jnp.zeros_like(rows)], axis=1)
    missing = HEAD_DIM - rows.shape[0] % HEAD_DIM
    if missing < HEAD_DIM:
        rows = jnp.concatenate([rows, jnp.zeros((missing, rows.shape[1]), jnp.float32)], axis=0)
    return jnp.transpose(rows)


def merge_kernel(steps, block_ref, *refs):
    count = len(steps)
    parts, (base_ref, top_ref, total_ref) = refs[:count], refs[count : count + 3]
    sum_refs = refs[count + 3 :]
    tokens, blocks, width = base_ref.shape
    size = TILE * tokens
    part = TILE * HEAD_DIM
    kv_heads = width // part
    top_ref[...] = jnp.full(top_ref.shape, -1e30, jnp.float32)
    total_ref[...] = jnp.zeros(total_ref.shape, jnp.float32)
    for sum_ref in sum_refs:
        sum_ref[...] = jnp.zeros(sum_ref.shape, jnp.float32)
    asking = [block_ref[step] for step in steps]
    logs = [unpack_logs(parts[n], kv_heads) for n in range(count)]
    for n in range(count):
        top_ref[asking[n]] = jnp.maximum(top_ref[asking[n]], logs[n])
    shares = [jnp.exp(logs[n] - top_ref[asking[n]]) for n in range(count)]
    for n in range(count):
        total_ref[asking[n]] += shares[n]
    columns = as_columns([shares[n] / total_ref[asking[n]] for n in range(count)])
    for n in range(count):
        for head, sum_ref in enumerate(sum_refs):
            place = n * kv_heads + head
            share = columns[:size, place : place + 1]
            part_rows = parts[n][head * size : (head + 1) * size, :]
            sum_ref[asking[n]] += share * part_rows.astype(jnp.float32)
    row = lax.broadcasted_iota(jnp.int32, (tokens * blocks, tokens * blocks), 0)
    column = lax.broadcasted_iota(jnp.int32, (tokens * blocks, tokens * blocks), 1)
    turned = (row // blocks == column % tokens) & (row % blocks == column // tokens)
    turn = jnp.where(turned, 1.0, 0.0).astype(jnp.bfloat16)
    for head, sum_ref in enumerate(sum_refs):
        span = slice(head * part, (head + 1) * part)
        lanes = [
            jnp.concatenate(
                [sum_ref[b, g * tokens : (g + 1) * tokens, :] for b in range(blocks)], axis=0
            )
            for g in range(TILE)
        ]
        block_rows = jnp.concatenate(lanes, axis=1).astype(jnp.bfloat16)
        token_rows = jnp.dot(turn, block_rows, preferred_element_type=jnp.float32)
        for t in range(tokens):
            base_ref[t, :, span] = token_rows[t * blocks : (t + 1) * blocks].astype(jnp.bfloat16)


def merge_pages(block_of, steps, parts, like):
    count = len(steps)
    tokens, blocks, width = like.shape
    kv_heads = width // (TILE * HEAD_DIM)
    size = TILE * tokens
    vmem = pl.BlockSpec(memory_space=pltpu.VMEM)
    stats = jax.ShapeDtypeStruct((blocks, kv_heads, size), jnp.float32)
    sums = jax.ShapeDtypeStruct((blocks, size, HEAD_DIM), jnp.float32)
    return pl.pallas_call(
        functools.partial(merge_kernel, steps),
        out_shape=[jax.ShapeDtypeStruct(like.shape, jnp.bfloat16), stats, stats]
        + [sums] * kv_heads,
        in_specs=[pl.BlockSpec(memory_space=pltpu.SMEM)] + [vmem] * count,
        out_specs=[vmem] * (3 + kv_heads),
        compiler_params=pltpu.CompilerParams(vmem_limit_bytes=VMEM_BYTES),
        cost_estimate=pl.CostEstimate(flops=0, bytes_accessed=4 << 20, transcendentals=0),
        name="merge_pages",
    )(block_of, *[parts[step] for step in steps])


def settle_kernel(steps, block_ref, base_ref, top_ref, total_ref, *refs):
    count = len(steps)
    parts, sum_refs = refs[:count], refs[count:-3]
    out_ref, done_ref, leaving = refs[-3:]
    tokens, blocks, width = out_ref.shape
    size = TILE * tokens
    part = TILE * HEAD_DIM
    kv_heads = width // part
    asking = [block_ref[step] for step in steps]
    logs = [unpack_logs(ref, kv_heads) for ref in parts]
    shares = []
    for block in asking:
        old = top_ref[block]
        own = [jnp.where(asking[n] == block, logs[n], -1e30) for n in range(count)]
        top = functools.reduce(jnp.maximum, own, old)
        weights = [jnp.exp(old - top) * total_ref[block]] + [jnp.exp(log - top) for log in own]
        total = sum(weights)
        shares += [weight / total for weight in weights]
    columns = as_columns(shares)
    row = lax.broadcasted_iota(jnp.int32, (tokens * blocks, count * tokens), 0)
    column = lax.broadcasted_iota(jnp.int32, (tokens * blocks, count * tokens), 1)
    turned = jnp.zeros(row.shape, jnp.bool_)
    block_row = lax.broadcasted_iota(jnp.int32, (blocks, part), 0)
    fresh = jnp.zeros((blocks, part), jnp.bool_)
    for n, block in enumerate(asking):
        first = jnp.bool_(True)
        for m in range(n):
            first = first & (asking[m] != block)
        wanted = jnp.where(first, block, -1)
        turned = turned | (
            (row // blocks == column - n * tokens) & (row % blocks == wanted)
        )
        fresh = fresh | (block_row == block)
    turn = jnp.where(turned, 1.0, 0.0).astype(jnp.bfloat16)
    copies = []
    for head, sum_ref in enumerate(sum_refs):
        span = slice(head * part, (head + 1) * part)
        merged = []
        for n, block in enumerate(asking):
            rows = [sum_ref[block]]
            rows += [ref[head * size : (head + 1) * size, :].astype(jnp.float32) for ref in parts]
            total = None
            for m, value in enumerate(rows):
                place = (n * (count + 1) + m) * kv_heads + head
                term = columns[:size, place : place + 1] * value
                total = term if total is None else total + term
            merged.append(total)
        lanes = [
            jnp.concatenate([rows[g * tokens : (g + 1) * tokens, :] for rows in merged], axis=0)
            for g in range(TILE)
        ]
        block_rows = jnp.concatenate(lanes, axis=1).astype(jnp.bfloat16)
        token_rows = jnp.dot(turn, block_rows, preferred_element_type=jnp.float32)
        for t in range(tokens):
            new = token_rows[t * blocks : (t + 1) * blocks]
            old = base_ref[t, :, span].astype(jnp.float32)
            done_ref[t, :, span] = jnp.where(fresh, new, old).astype(jnp.bfloat16)
        copy = pltpu.make_async_copy(
            done_ref.at[:, :, span], out_ref.at[:, :, span], leaving.at[head]
        )
        copy.start()
        copies.append(copy)
    for copy in copies:
        copy.wait()


def settle_pages(block_of, merged, steps, parts):
    count = len(steps)
    base, top, total, *sums = merged
    vmem = pl.BlockSpec(memory_space=pltpu.VMEM)
    return pl.pallas_call(
        functools.partial(settle_kernel, steps),
        out_shape=jax.ShapeDtypeStruct(base.shape, jnp.bfloat16),
        in_specs=[pl.BlockSpec(memory_space=pltpu.SMEM)] + [vmem] * (3 + count + len(sums)),
        out_specs=pl.BlockSpec(memory_space=pltpu.HBM),
        scratch_shapes=[
            pltpu.VMEM(base.shape, jnp.bfloat16),
            pltpu.SemaphoreType.DMA((len(sums),)),
        ],
        compiler_params=pltpu.CompilerParams(vmem_limit_bytes=VMEM_BYTES),
        cost_estimate=pl.CostEstimate(flops=0, bytes_accessed=4 << 20, transcendentals=0),
        name="settle_pages",
    )(block_of, base, top, total, *[parts[step] for step in steps], *sums)


class Window:
    def __init__(self, far, depth):
        self.far, self.depth = far, depth
        self.arrived = {False: [], True: []}

    def swap(self, value, step):
        if step == 0:
            return value
        arrived = self.arrived[step >= self.far]
        if len(arrived) >= self.depth:
            value, _ = lax.optimization_barrier((value, arrived[-self.depth]))
        count = lax.axis_size("ctx")
        pairs = [(source, source ^ step) for source in range(count)]
        arrived.append(lax.ppermute(value, "ctx", pairs))
        return arrived[-1]


def stepped_body(queries, kv_cache, page_counts, doc_ids):
    every = tuple(range(lax.axis_size("ctx")))
    early = (8, 9)
    late = tuple(step for step in every if step not in early)
    _, first = pack_queries(queries, page_counts, doc_ids, early, early)
    block_of, rest = pack_queries(queries, page_counts, doc_ids, late, every)
    sent = dict(zip(early + late, first + rest))
    window = Window(len(every) // 2, 3)
    asked, parts = {}, {}

    def ask(*steps):
        for step in steps:
            asked[step] = window.swap(sent[step], step)

    def attend(*steps):
        for step, part in zip(steps, attend_page(kv_cache[0], [asked[s] for s in steps])):
            parts[step] = part

    def answer(*steps):
        for step in steps:
            parts[step] = window.swap(parts[step], step)

    ask(8, 9, 1, 10, 11, 2, 4, 12, 13, 3, 14, 5, 15, 6, 7, 0)
    attend(0, 1, 2, 3)
    attend(8, 9, 10, 11)
    answer(8, 9, 1, 10, 2)
    attend(4, 5, 6, 7)
    answer(11, 4, 3)
    attend(12, 13, 14, 15)
    answer(12, 5, 13, 6, 7, 14, 15)
    last = (14, 15)
    before = tuple(step for step in every if step not in last)
    merged = merge_pages(block_of, before, parts, queries)
    return settle_pages(block_of, merged, last, parts)


def body(queries, kv_cache, page_counts, doc_ids):
    tokens, blocks, width = queries.shape
    groups = width // kv_cache.shape[-1]
    fits = tokens == TILE and blocks == TILE and groups == TILE and lax.axis_size("ctx") == 2 * TILE
    chosen = stepped_body if fits else gathered_body
    return chosen(queries, kv_cache, page_counts, doc_ids)


def solution(mesh):
    placed = (
        P(("group", "ctx"), None, None),
        P(("group", "ctx"), None, None, None),
        P("group"),
        P("group"),
    )
    return jax.shard_map(
        body, mesh=mesh, in_specs=placed, out_specs=P(("group", "ctx"), None, None), check_vma=False
    )
```
